128 devices in a mesh: gx: 8 (over y, core), gy: 16 (over x, z).
Axes of the slice: x: 4, y: 4, z: 4, core: 2. Of those that a mesh axis runs over, the one named last changes fastest.
Arguments:
- ocean_state: float32 [2048, 4, 32, 128], P(('gx', 'gy')), may hold values from -3 to 3
- land_mask: int32 [2048, 32, 128], P(('gx', 'gy')), may hold values 0 or 1
- ocean_map: int32 [2048], P(('gx', 'gy')), may hold values from 0 to 2047, as said below
- ice_motion: float32 [2048, 5, 32, 128], P(('gx', 'gy')), may hold values from -3 to 3
- ice_mass: float32 [2048, 32, 128], P(('gx', 'gy')), may hold values from 0.5 to 2
- ice_strength: float32 [2048, 32, 128], P(('gx', 'gy')), may hold values from 0.5 to 2
- ice_mask: int32 [2048, 32, 128], P(('gx', 'gy')), may hold values 0 or 1
- ice_map: int32 [2048], P(('gx', 'gy')), may hold values from 0 to 2047, as said below
Outputs:
- ice_result: float32 [2048, 5, 32, 128], P(('gx', 'gy'))
- ocean_stress: float32 [2048, 2, 32, 128], P(('gx', 'gy'))
The draws below stay inside these ranges and needn't reach their ends.
Inputs may be any that keep to these rules, and one draw needn't show every extreme that they name: ocean_map and ice_map each name every block once. The 16 slots of device (gx, gy) hold blocks of block rows gx * 1 to gx + 1 - 1 only, and for every c exactly 1 of them lie in block columns c * 16 to c * 16 + 15. `ice_map`: as for ocean_map, drawn independently.
All inputs are finite; a program needn't handle non-finite values. No bound on the sum of `land_mask` or of `ice_mask` on one device may be relied on, other than what follows from the above.
Results may differ from the reference program's by a relative error of at most 0.00019.
Values sent between devices are 32-bit elements; how exact they have to be, the bound alone decides.
A program may use at most 192 MiB of HBM per device.

```python
import math
import jax
import jax.numpy as jnp

BH = 32
BW = 128
RB = 1
CB = 16
ITERS = 8
BPD = 16
NB = 2048
NR = 256
NC = 32768
N_GX = 8
N_GY = 16


def build_map(key):
    per_owner = BPD // N_GY
    ncols = N_GY * CB
    row_index = jnp.arange(N_GX, dtype=jnp.int32)[:, None, None]
    owner_index = jnp.arange(N_GY, dtype=jnp.int32)[None, :, None]
    block_slot = jnp.arange(BPD, dtype=jnp.int32)[None, None, :]
    block_ids = (row_index * RB + block_slot // CB) * ncols + owner_index * CB + block_slot % CB
    key_list = jax.random.split(jax.random.fold_in(key, 11), N_GX * N_GY)
    shuffle = jax.vmap(lambda subkey: jax.random.permutation(subkey, BPD))(key_list).reshape(N_GX, N_GY, BPD)
    block_ids = jnp.take_along_axis(block_ids, shuffle, axis=2).reshape(N_GX, N_GY, N_GY, per_owner)
    key_list = jax.random.split(jax.random.fold_in(key, 12), N_GX * N_GY)
    target_col = jax.vmap(lambda subkey: jax.random.permutation(subkey, N_GY))(key_list).reshape(N_GX, N_GY, N_GY)
    inverse = jnp.argsort(target_col, axis=2).astype(jnp.int32)
    picked = jnp.take_along_axis(block_ids, inverse[..., None], axis=2)
    received = picked.transpose(0, 2, 1, 3).reshape(N_GX, N_GY, BPD)
    key_list = jax.random.split(jax.random.fold_in(key, 13), N_GX * N_GY)
    shuffle = jax.vmap(lambda subkey: jax.random.permutation(subkey, BPD))(key_list).reshape(N_GX, N_GY, BPD)
    received = jnp.take_along_axis(received, shuffle, axis=2)
    return received.reshape(NB).astype(jnp.int32)


def draw_ocean_map(key, part):
    key = jax.random.fold_in(key, 1)
    return build_map(key)


def draw_ice_map(key, part):
    key = jax.random.fold_in(key, 2)
    return build_map(key)


def plant(drawn, stream_key, smallest, high):
    longest = drawn.shape.index(max(drawn.shape))
    spots = []
    for shift in (0, 1):
        where = [jax.random.randint(jax.random.fold_in(stream_key, axis), (), 0, length) for axis, length in enumerate(drawn.shape)]
        where[longest] = (where[longest] + shift) % drawn.shape[longest]
        spots.append(tuple(where))
    return drawn.at[spots[0]].set(smallest).at[spots[1]].set(high)


def block_levels(key, extent, shards, least, largest):
    level = 1.0
    for dim, parts in shards:
        steps = jax.random.uniform(jax.random.fold_in(jax.random.fold_in(key, 6), dim), (parts,), jnp.float32, least / len(shards), largest / len(shards))
        level = level * jnp.repeat(jnp.exp(steps), extent[dim] // parts).reshape((-1,) + (1,) * (len(extent) - 1 - dim))
    return level


def centred(own_key, shape, width, bound, cuts=(), kind=jnp.bfloat16):
    values = width * jax.random.normal(own_key, shape, jnp.float32)
    if cuts:
        values = values * block_levels(own_key, shape, cuts, -0.22, 0.18)
    return jnp.clip(values, -bound, bound).astype(kind)


def setup_inputs(seed: int = 0) -> dict:
    streams_of = jax.random.split(jax.random.key(seed), 9)
    return {
        "ocean_state": centred(streams_of[0], (NB, 4, BH, BW), 0.5, 3.0, ((0, 128),), jnp.float32),
        "land_mask": plant((jax.random.randint(streams_of[1], (NB, BH, BW), 0, 8) < 1).astype(jnp.int32), jax.random.fold_in(streams_of[1], 1), 0, 1),
        "ocean_map": draw_ocean_map(jax.random.fold_in(streams_of[8], 71), 0),
        "ice_motion": centred(streams_of[3], (NB, 5, BH, BW), 0.5, 3.0, ((0, 128),), jnp.float32),
        "ice_mass": jnp.clip(jnp.exp(math.log(2.0) - 1.3862944 * jax.random.uniform(streams_of[4], (NB, BH, BW), jnp.float32) ** block_levels(streams_of[4], (NB, BH, BW), ((0, 128),), -0.2, 0.2)), 0.5, 2.0),
        "ice_strength": jnp.clip(jnp.exp(math.log(2.0) - 1.3862944 * jax.random.uniform(streams_of[5], (NB, BH, BW), jnp.float32) ** block_levels(streams_of[5], (NB, BH, BW), ((0, 128),), -0.2, 0.2)), 0.5, 2.0),
        "ice_mask": plant((jax.random.randint(streams_of[6], (NB, BH, BW), 0, 4) < 3).astype(jnp.int32), jax.random.fold_in(streams_of[6], 1), 0, 1),
        "ice_map": draw_ice_map(jax.random.fold_in(streams_of[8], 71), 0),
    }


ECC_SQ = 4.0
RELAX = 1.5
DELTA_MIN_SQ = 0.04
CORIOLIS = 0.5
DRAG_FLOOR = 0.01

def along_x(padded):
    return 0.5 * (padded[..., 1:-1, 2:] - padded[..., 1:-1, :-2])

def along_y(padded):
    return 0.5 * (padded[..., 2:, 1:-1] - padded[..., :-2, 1:-1])

def stress_update(vel_pad, stresses, strength):
    east = along_x(vel_pad[0])
    north = along_y(vel_pad[1])
    shear = along_y(vel_pad[0]) + along_x(vel_pad[1])
    diverg = east + north
    tension = east - north
    delta = jnp.sqrt(diverg * diverg + (tension * tension + shear * shear) / ECC_SQ + DELTA_MIN_SQ)
    ratio = 0.5 * strength / delta
    target = jnp.stack([ratio * diverg - 0.5 * strength, ratio * tension / ECC_SQ, 0.5 * ratio * shear / ECC_SQ])
    return (stresses + RELAX * target) / (1.0 + RELAX)

def divergence(stress_pad):
    normal_xx = 0.5 * (stress_pad[0] + stress_pad[1])
    normal_yy = 0.5 * (stress_pad[0] - stress_pad[1])
    force_x = along_x(normal_xx) + along_y(stress_pad[2])
    force_y = along_x(stress_pad[2]) + along_y(normal_yy)
    return (force_x, force_y)

def momentum(velocity, force_x, force_y, mass, active, forcing):
    diff_x = forcing[0] - velocity[0]
    diff_y = forcing[1] - velocity[1]
    cdrag = jnp.sqrt(diff_x * diff_x + diff_y * diff_y + DRAG_FLOOR)
    diag = mass + cdrag
    rotate = CORIOLIS * mass
    rhs_x = mass * velocity[0] + force_x + cdrag * forcing[0] - mass * forcing[2]
    rhs_y = mass * velocity[1] + force_y + cdrag * forcing[1] - mass * forcing[3]
    determ = diag * diag + rotate * rotate
    new_x = active * (diag * rhs_x + rotate * rhs_y) / determ
    new_y = active * (diag * rhs_y - rotate * rhs_x) / determ
    return jnp.stack([new_x, new_y])

def drag_stress(velocity, forcing, active):
    diff_x = velocity[0] - forcing[0]
    diff_y = velocity[1] - forcing[1]
    cdrag = active * jnp.sqrt(diff_x * diff_x + diff_y * diff_y + DRAG_FLOOR)
    return jnp.stack([cdrag * diff_x, cdrag * diff_y])

def to_grid(blocks, block_ids):
    by_block = jnp.zeros_like(blocks).at[block_ids].set(blocks)
    fields = blocks.shape[1]
    shaped = by_block.reshape(N_GX * RB, N_GY * CB, fields, BH, BW)
    return shaped.transpose(2, 0, 3, 1, 4).reshape(fields, NR, NC)

def to_blocks(field, block_ids):
    fields = field.shape[0]
    shaped = field.reshape(fields, N_GX * RB, BH, N_GY * CB, BW).transpose(1, 3, 0, 2, 4)
    return shaped.reshape(NB, fields, BH, BW)[block_ids]

def pad_one(field):
    return jnp.pad(field, ((0, 0), (1, 1), (1, 1)))

def reference(ocean_state, land_mask, ocean_map, ice_motion, ice_mass, ice_strength, ice_mask, ice_map):
    forcing = to_grid(ocean_state, ocean_map)
    land = to_grid(land_mask.astype(jnp.float32)[:, None], ocean_map)[0]
    motion = to_grid(ice_motion, ice_map)
    mass = to_grid(ice_mass[:, None], ice_map)[0]
    strength = to_grid(ice_strength[:, None], ice_map)[0]
    covered = to_grid(ice_mask.astype(jnp.float32)[:, None], ice_map)[0]
    active = covered * (1.0 - land)
    velocity = motion[0:2]
    stresses = motion[2:5]
    for step in range(ITERS):
        stresses = stress_update(pad_one(velocity), stresses, strength)
        force_x, force_y = divergence(pad_one(stresses))
        velocity = momentum(velocity, force_x, force_y, mass, active, forcing)
    ice_result = to_blocks(jnp.concatenate([velocity, stresses], axis=0), ice_map)
    ocean_stress = to_blocks(drag_stress(velocity, forcing, active), ocean_map)
    return (ice_result, ocean_stress)
```

```python
import functools

import jax
import jax.numpy as jnp
from jax import lax
from jax.experimental import pallas as pl
from jax.experimental.pallas import tpu as pltpu
from jax.sharding import PartitionSpec as P

BH = 32
BW = 128
NP = 16
NX = 8
ITERS = 8
DEEP = 16
HIGH = BH + 2 * DEEP
NBLK = NP + 1
EDGE = 8
ROWS = HIGH + 2 * EDGE
MESH = pl.DeviceIdType.MESH
F32 = jnp.float32

GROUPS = (
    (("u", "i"), ("v", "i"), ("p", "i")),
    (("s1", "i"), ("s2", "i"), ("s12", "i")),
    (("m", "i"), ("uo", "o"), ("vo", "o")),
    (("tx", "o"), ("ty", "o"), ("ac", "o")),
)
NG = len(GROUPS)
PER = 3
SIDE_SETS = (("u", "v", "p", "s1", "s2", "s12"), ("m", "uo", "vo", "tx", "ty", "ac"))
TILE_FIELDS = ("u", "v", "p", "s1", "s2", "s12", "m", "uo", "vo", "tx", "ty", "ac", "sa", "sc")


def shifted(col, k, sign):
    dx, dz = lax.div(k, 4), lax.rem(k, 4)
    x, z = lax.div(col, 4), lax.rem(col, 4)
    return lax.rem(x + sign * dx + 4, 4) * 4 + lax.rem(z + sign * dz + 4, 4)


def tile_col(block_id):
    return lax.rem(lax.div(block_id, NP), NP)


def x_difference(ref, off, j, lane):
    sl = pl.ds(EDGE + off, 8)
    here = ref[j, sl]
    up = pltpu.roll(jnp.where(lane == 0, ref[(j + 1) % NBLK, sl], here), BW - 1, 1)
    down = pltpu.roll(jnp.where(lane == BW - 1, ref[(j - 1) % NBLK, sl], here), 1, 1)
    return up - down


def y_difference(ref, off, j):
    return ref[j, pl.ds(EDGE + off + 1, 8)] - ref[j, pl.ds(EDGE + off - 1, 8)]


def stress_rows(t, off, j, lane):
    sl = pl.ds(EDGE + off, 8)
    east = x_difference(t["u"], off, j, lane)
    north = y_difference(t["v"], off, j)
    shear = y_difference(t["u"], off, j) + x_difference(t["v"], off, j, lane)
    diverg = east + north
    tension = east - north
    square = diverg * diverg + (tension * tension + shear * shear) * 0.25 + 0.16
    p = t["p"][j, sl]
    ratio = p * lax.rsqrt(square)
    s1 = 0.4 * t["s1"][j, sl] + (ratio * diverg - p)
    s2 = 0.4 * t["s2"][j, sl] + ratio * tension
    s12 = 0.4 * t["s12"][j, sl] + ratio * shear
    quarter = 0.25 * s2
    t["s1"][j, sl] = s1
    t["s2"][j, sl] = s2
    t["s12"][j, sl] = s12
    t["sa"][j, sl] = s1 + quarter
    t["sc"][j, sl] = s1 - quarter


def momentum_rows(t, off, j, lane):
    sl = pl.ds(EDGE + off, 8)
    force_x = x_difference(t["sa"], off, j, lane) * 0.25 + y_difference(t["s12"], off, j) * 0.0625
    force_y = x_difference(t["s12"], off, j, lane) * 0.0625 + y_difference(t["sc"], off, j) * 0.25
    u, v, m = t["u"][j, sl], t["v"][j, sl], t["m"][j, sl]
    uo, vo = t["uo"][j, sl], t["vo"][j, sl]
    diff_x, diff_y = uo - u, vo - v
    square = diff_x * diff_x + diff_y * diff_y + 0.01
    drag = square * lax.rsqrt(square)
    diag = m + drag
    rotate = 0.5 * m
    rhs_x = m * (u - t["tx"][j, sl]) + force_x + drag * uo
    rhs_y = m * (v - t["ty"][j, sl]) + force_y + drag * vo
    scale = t["ac"][j, sl] * pltpu.reciprocal(diag * diag + rotate * rotate, approx=True)
    t["u"][j, sl] = (diag * rhs_x + rotate * rhs_y) * scale
    t["v"][j, sl] = (diag * rhs_y - rotate * rhs_x) * scale


def body(
    omap, imap, ocean_h, land_h, motion_h, mass_h, strength_h, mask_h,
    ice_out, ocean_out,
    ocean, land, motion, mass, strength, mask,
    send, recv, top, bottom, ids_send, ids_recv, ids_top, ids_bottom, order_v, inverse_v,
    order, inverse, side_send, side_recv, back_ice, back_ocean, tile,
    in_sem, id_s, id_r, idf_s, idf_r, small_sem, data_s, data_r,
    top_s, top_r, bot_s, bot_r, side_s, side_r, back_s, back_r, own_sem,
):
    gx, gy = lax.axis_index("gx"), lax.axis_index("gy")
    t = dict(zip(TILE_FIELDS, tile))
    lane = lax.broadcasted_iota(jnp.int32, (8, BW), 1)
    row8 = lax.broadcasted_iota(jnp.int32, (8, BW), 0)

    barrier = pltpu.get_barrier_semaphore()

    def greet(k, _):
        pl.semaphore_signal(barrier, inc=1, device_id=(gx, shifted(gy, k, 1)), device_id_type=MESH)
        return 0

    lax.fori_loop(1, NP, greet, 0)
    for d in (1, NX - 1):
        pl.semaphore_signal(
            barrier, inc=1, device_id=(lax.rem(gx + d, NX), gy), device_id_type=MESH
        )
    loads = [
        pltpu.make_async_copy(motion_h, motion, in_sem.at[0]),
        pltpu.make_async_copy(strength_h, strength, in_sem.at[1]),
        pltpu.make_async_copy(mass_h, mass, in_sem.at[2]),
        pltpu.make_async_copy(mask_h, mask, in_sem.at[3]),
        pltpu.make_async_copy(ocean_h, ocean, in_sem.at[4]),
        pltpu.make_async_copy(land_h, land, in_sem.at[5]),
    ]
    for load in loads:
        load.start()

    tile_of = lax.broadcasted_iota(jnp.int32, (NP, NP), 0)
    slot_of = lax.broadcasted_iota(jnp.int32, (NP, NP), 1)
    places = []
    for row, blocks in ((0, imap), (1, omap)):
        block = jnp.broadcast_to(blocks[...], (NP, NP))
        same = tile_col(block) == tile_of
        slot = jnp.max(jnp.where(same, slot_of, 0), axis=1, keepdims=True)
        place_in = jnp.max(jnp.where(same, lax.rem(block, NP), 0), axis=1, keepdims=True)
        order_v[row] = jnp.broadcast_to(slot, (NP, BW))
        places.append(jnp.broadcast_to(place_in, (NP, BW)))
    order_copy = pltpu.make_async_copy(order_v, order, small_sem.at[0])
    order_copy.start()
    for c in range(NP):
        ids_send[c] = jnp.where(row8 == 0, places[0][c : c + 1], places[1][c : c + 1])
    ids_recv[0] = ids_send[gy]
    order_copy.wait()

    def packed(name, si, so):
        if name == "p":
            return strength[si] * 0.3
        if name == "m":
            return mass[si] * mask[si].astype(F32)
        if name == "ac":
            return (1 - land[so]).astype(F32)
        if name in ("u", "v", "s1"):
            return motion[si, ("u", "v", "s1").index(name)]
        if name == "s2":
            return motion[si, 3] * 4.0
        if name == "s12":
            return motion[si, 4] * 8.0
        return ocean[so, ("uo", "vo", "tx", "ty").index(name)]

    def pack(g):
        def one(k, _):
            c = shifted(gy, k, 1)
            si, so = order[0, c, 0], order[1, c, 0]
            for f, (name, _kind) in enumerate(GROUPS[g]):
                send[g, k, f] = packed(name, si, so)
            return 0

        lax.fori_loop(1, NP, one, 0)
        si, so = order[0, gy, 0], order[1, gy, 0]
        for f, (name, _kind) in enumerate(GROUPS[g]):
            recv[g][0, f] = packed(name, si, so)

    def data_copy(g, k):
        return pltpu.make_async_remote_copy(
            src_ref=send.at[g, k], dst_ref=recv[g].at[k],
            send_sem=data_s.at[g, k], recv_sem=data_r.at[g, k],
            device_id=(gx, shifted(gy, k, 1)), device_id_type=MESH,
        )

    def id_copy(k):
        return pltpu.make_async_remote_copy(
            src_ref=ids_send.at[shifted(gy, k, 1)], dst_ref=ids_recv.at[k],
            send_sem=id_s.at[k], recv_sem=id_r.at[k],
            device_id=(gx, shifted(gy, k, 1)), device_id_type=MESH,
        )

    def top_copy(g, k):
        return pltpu.make_async_remote_copy(
            src_ref=recv[g].at[k, :, pl.ds(DEEP, DEEP)], dst_ref=top[g].at[k],
            send_sem=top_s.at[g, k], recv_sem=top_r.at[g, k],
            device_id=(gx + 1, gy), device_id_type=MESH,
        )

    def bottom_copy(g, k):
        return pltpu.make_async_remote_copy(
            src_ref=recv[g].at[k, :, pl.ds(0, DEEP)], dst_ref=bottom[g].at[k],
            send_sem=bot_s.at[g, k], recv_sem=bot_r.at[g, k],
            device_id=(gx - 1, gy), device_id_type=MESH,
        )

    def id_forward(d):
        return pltpu.make_async_remote_copy(
            src_ref=ids_recv, dst_ref=(ids_top, ids_bottom)[d],
            send_sem=idf_s.at[d], recv_sem=idf_r.at[d],
            device_id=((gx + 1, gx - 1)[d], gy), device_id_type=MESH,
        )

    def each(lo, fn):
        def step(k, _):
            fn(k)
            return 0

        lax.fori_loop(lo, NP, step, 0)

    loads[0].wait()
    loads[1].wait()
    pack(0)
    pl.semaphore_wait(barrier, NP - 1 + 2)
    each(1, lambda k: id_copy(k).start())
    each(1, lambda k: data_copy(0, k).start())
    pack(1)
    each(1, lambda k: data_copy(1, k).start())
    for load in loads[2:5]:
        load.wait()
    pack(2)
    each(1, lambda k: data_copy(2, k).start())
    loads[5].wait()
    pack(3)
    each(1, lambda k: data_copy(3, k).start())

    @pl.when(gx == 0)
    def _():
        ids_top[...] = jnp.zeros(ids_top.shape, jnp.int32)

        def clear(k):
            for g in range(NG):
                top[g][k] = jnp.zeros((PER, DEEP, BW), F32)

        each(0, clear)

    @pl.when(gx == NX - 1)
    def _():
        ids_bottom[...] = jnp.zeros(ids_bottom.shape, jnp.int32)

        def clear(k):
            for g in range(NG):
                bottom[g][k] = jnp.zeros((PER, DEEP, BW), F32)

        each(0, clear)

    for e in range(2):

        @pl.when(gy == (0, NP - 1)[e])
        def _():
            side_recv[:, e] = jnp.zeros((2, HIGH, BW), F32)

    for name in TILE_FIELDS:
        t[name][:, pl.ds(0, EDGE)] = jnp.zeros((NBLK, EDGE, BW), F32)
        t[name][:, pl.ds(ROWS - EDGE, EDGE)] = jnp.zeros((NBLK, EDGE, BW), F32)

    each(1, lambda k: id_copy(k).wait_recv())

    @pl.when(gx < NX - 1)
    def _():
        id_forward(0).start()

    @pl.when(gx > 0)
    def _():
        id_forward(1).start()

    def invert(which, source):
        found = jnp.zeros((8, BW), jnp.int32)
        for k in range(NP):
            found = jnp.maximum(found, jnp.where(source[k] == lane, k, 0))
        inverse_v[which] = found
        copy = pltpu.make_async_copy(inverse_v.at[which], inverse.at[which], small_sem.at[1 + which])
        copy.start()
        copy.wait()

    invert(0, ids_recv)
    place_of = jnp.zeros((8, BW), jnp.int32)
    for k in range(NP):
        place_of = jnp.where(lane == k, ids_recv[k], place_of)
    inverse_v[3] = place_of
    place_copy = pltpu.make_async_copy(inverse_v.at[3], inverse.at[3], small_sem.at[4])
    place_copy.start()
    place_copy.wait()

    @pl.when(gx > 0)
    def _():
        id_forward(0).wait_recv()

    invert(1, ids_top)

    @pl.when(gx < NX - 1)
    def _():
        id_forward(1).wait_recv()

    invert(2, ids_bottom)

    def forward(g, k):
        @pl.when(gx < NX - 1)
        def _():
            top_copy(g, k).start()

        @pl.when(gx > 0)
        def _():
            bottom_copy(g, k).start()

    def place(g, which, source, row, rows):
        def one(j):
            for f, (name, kind) in enumerate(GROUPS[g]):
                src = inverse[which, "io".index(kind), j]
                sl = pl.ds(EDGE + row, rows)
                value = source[src, f]
                if name == "ac":
                    value = jnp.where(t["m"][j, sl] > 0.0, value, 0.0)
                t[name][j, sl] = value

        each(0, one)

    def place_halo(g):
        @pl.when(gx > 0)
        def _():
            each(0, lambda k: top_copy(g, k).wait_recv())

        @pl.when(gx < NX - 1)
        def _():
            each(0, lambda k: bottom_copy(g, k).wait_recv())

        place(g, 1, top[g], 0, DEEP)
        place(g, 2, bottom[g], DEEP + BH, DEEP)

    def side_copy(n, e):
        return pltpu.make_async_remote_copy(
            src_ref=side_send.at[n, e], dst_ref=side_recv.at[n, e],
            send_sem=side_s.at[n, e], recv_sem=side_r.at[n, e],
            device_id=(gx, (gy + 1, gy - 1)[e]), device_id_type=MESH,
        )

    def send_sides(n):
        for a in range(HIGH // 8):
            right = jnp.zeros((8, BW), F32)
            left = jnp.zeros((8, BW), F32)
            for f, name in enumerate(SIDE_SETS[n]):
                here = (lane >= DEEP * f) & (lane < DEEP * (f + 1))
                r = t[name][NP - 1, pl.ds(EDGE + 8 * a, 8)]
                q = t[name][0, pl.ds(EDGE + 8 * a, 8)]
                right = jnp.where(here, pltpu.roll(r, (DEEP * f + DEEP) % BW, 1), right)
                left = jnp.where(here, pltpu.roll(q, DEEP * f, 1) if f else q, left)
            side_send[n, 0, pl.ds(8 * a, 8)] = right
            side_send[n, 1, pl.ds(8 * a, 8)] = left

        @pl.when(gy < NP - 1)
        def _():
            side_copy(n, 0).start()

        @pl.when(gy > 0)
        def _():
            side_copy(n, 1).start()

    def take_sides(n):
        @pl.when(gy > 0)
        def _():
            side_copy(n, 0).wait_recv()

        @pl.when(gy < NP - 1)
        def _():
            side_copy(n, 1).wait_recv()

        for a in range(HIGH // 8):
            left = side_recv[n, 0, pl.ds(8 * a, 8)]
            right = side_recv[n, 1, pl.ds(8 * a, 8)]
            for f, name in enumerate(SIDE_SETS[n]):
                r = pltpu.roll(right, BW - DEEP * f, 1) if f else right
                q = pltpu.roll(left, BW - DEEP - DEEP * f, 1)
                value = jnp.where(lane < DEEP, r, jnp.where(lane >= BW - DEEP, q, 0.0))
                t[name][NP, pl.ds(EDGE + 8 * a, 8)] = value

    def arrive(g):
        def one(k):
            data_copy(g, k).wait_recv()
            forward(g, k)

        forward(g, 0)
        each(1, one)
        place(g, 0, recv[g], DEEP, BH)

    arrive(0)
    arrive(1)
    place_halo(0)
    arrive(2)
    place_halo(1)
    send_sides(0)
    arrive(3)
    place_halo(2)
    place_halo(3)
    send_sides(1)
    take_sides(0)
    take_sides(1)

    def subcycle(n, _):
        skip_s, skip_m = lax.div(n, 4), lax.div(n + 1, 4)

        def stress_step(i, _):
            for a in range(2):
                off = (skip_s + 2 * i + a) * 8
                for j in range(NBLK):
                    stress_rows(t, off, j, lane)
            return 0

        lax.fori_loop(0, 4 - skip_s, stress_step, 0)

        def momentum_step(i, _):
            for a in range(2):
                off = (skip_m + 2 * i + a) * 8
                for j in range(NBLK):
                    momentum_rows(t, off, j, lane)
            return 0

        lax.fori_loop(0, 4 - skip_m, momentum_step, 0)
        return 0

    lax.fori_loop(0, ITERS, subcycle, 0)

    def back_copy(part, k):
        src, dst = (
            (back_ice.at[k, pl.ds(2, 3)], ice_out.at[k, pl.ds(2, 3)]),
            (back_ice.at[k, pl.ds(0, 2)], ice_out.at[k, pl.ds(0, 2)]),
            (back_ocean.at[k], ocean_out.at[k]),
        )[part]
        return pltpu.make_async_remote_copy(
            src_ref=src, dst_ref=dst, send_sem=back_s.at[part, k], recv_sem=back_r.at[part, k],
            device_id=(gx, shifted(gy, k, -1)), device_id_type=MESH,
        )

    def mine(name, at):
        return t[name][at, pl.ds(EDGE + DEEP, BH)]

    def pack_stress(k):
        at = inverse[3, 0, k]
        back_ice[k, 2] = mine("s1", at)
        back_ice[k, 3] = mine("s2", at) * 0.25
        back_ice[k, 4] = mine("s12", at) * 0.125

    def pack_velocity(k):
        at = inverse[3, 0, k]
        back_ice[k, 0] = mine("u", at)
        back_ice[k, 1] = mine("v", at)

    def pack_ocean(k):
        at = inverse[3, 1, k]
        diff_x = mine("u", at) - mine("uo", at)
        diff_y = mine("v", at) - mine("vo", at)
        square = diff_x * diff_x + diff_y * diff_y + 0.01
        drag = mine("ac", at) * (square * lax.rsqrt(square))
        back_ocean[k, 0] = drag * diff_x
        back_ocean[k, 1] = drag * diff_y

    def give_back(part, fill):
        def one(k):
            fill(k)
            back_copy(part, k).start()

        each(1, one)
        fill(0)

    give_back(0, pack_stress)
    give_back(1, pack_velocity)
    give_back(2, pack_ocean)
    own_ice = pltpu.make_async_copy(back_ice.at[0], ice_out.at[0], own_sem.at[0])
    own_ocean = pltpu.make_async_copy(back_ocean.at[0], ocean_out.at[0], own_sem.at[1])
    own_ice.start()
    own_ocean.start()

    def drain(k):
        id_copy(k).wait_send()
        for g in range(NG):
            data_copy(g, k).wait_send()

    each(1, drain)

    @pl.when(gx < NX - 1)
    def _():
        id_forward(0).wait_send()

        def one(k):
            for g in range(NG):
                top_copy(g, k).wait_send()

        each(0, one)

    @pl.when(gx > 0)
    def _():
        id_forward(1).wait_send()

        def one(k):
            for g in range(NG):
                bottom_copy(g, k).wait_send()

        each(0, one)

    @pl.when(gy < NP - 1)
    def _():
        for n in range(2):
            side_copy(n, 0).wait_send()

    @pl.when(gy > 0)
    def _():
        for n in range(2):
            side_copy(n, 1).wait_send()

    own_ice.wait()
    own_ocean.wait()

    def finish(k):
        for part in range(3):
            back_copy(part, k).wait_recv()

    each(1, finish)

    def finish_send(k):
        for part in range(3):
            back_copy(part, k).wait_send()

    each(1, finish_send)


def to_slots(omap, imap, ice_in, ocean_in, ice_out, ocean_out, ice_sem, ocean_sem):
    gy = lax.axis_index("gy")
    x, z = lax.div(gy, 4), lax.rem(gy, 4)

    def copies(s):
        found = []
        for blocks in (imap, omap):
            c = tile_col(blocks[s])
            cx, cz = lax.div(c, 4), lax.rem(c, 4)
            found.append(lax.rem(cx - x + 4, 4) * 4 + lax.rem(cz - z + 4, 4))
        return (
            pltpu.make_async_copy(ice_in.at[found[0]], ice_out.at[s], ice_sem.at[s]),
            pltpu.make_async_copy(ocean_in.at[found[1]], ocean_out.at[s], ocean_sem.at[s]),
        )

    started = [copies(s) for s in range(NP)]
    for pair in started:
        for copy in pair:
            copy.start()
    for pair in started:
        for copy in pair:
            copy.wait()


def shards(ocean_state, land_mask, ocean_map, ice_motion, ice_mass, ice_strength, ice_mask, ice_map):
    dma = pltpu.SemaphoreType.DMA
    vmem = pltpu.VMEM
    hbm = pl.BlockSpec(memory_space=pl.ANY)
    smem = pl.BlockSpec(memory_space=pltpu.SMEM)
    back = (
        jax.ShapeDtypeStruct((NP, 5, BH, BW), F32),
        jax.ShapeDtypeStruct((NP, 2, BH, BW), F32),
    )
    ids = vmem((NP, 8, BW), jnp.int32)
    ice_back, ocean_back = pl.pallas_call(
        body,
        out_shape=back,
        in_specs=[pl.BlockSpec(memory_space=pltpu.VMEM)] * 2 + [hbm] * 6,
        out_specs=(hbm, hbm),
        scratch_shapes=[
            vmem((NP, 4, BH, BW), F32),
            vmem((NP, BH, BW), jnp.int32),
            vmem((NP, 5, BH, BW), F32),
            vmem((NP, BH, BW), F32),
            vmem((NP, BH, BW), F32),
            vmem((NP, BH, BW), jnp.int32),
            vmem((NG, NP, PER, BH, BW), F32),
            [vmem((NP, PER, BH, BW), F32) for _ in GROUPS],
            [vmem((NP, PER, DEEP, BW), F32) for _ in GROUPS],
            [vmem((NP, PER, DEEP, BW), F32) for _ in GROUPS],
            ids, ids, ids, ids,
            vmem((2, NP, BW), jnp.int32),
            vmem((4, 8, BW), jnp.int32),
            pltpu.SMEM((2, NP, BW), jnp.int32),
            pltpu.SMEM((4, 8, BW), jnp.int32),
            vmem((2, 2, HIGH, BW), F32),
            vmem((2, 2, HIGH, BW), F32),
            vmem((NP, 5, BH, BW), F32),
            vmem((NP, 2, BH, BW), F32),
            [vmem((NBLK, ROWS, BW), F32) for _ in TILE_FIELDS],
            dma((6,)), dma((NP,)), dma((NP,)), dma((2,)), dma((2,)), dma((5,)),
            dma((NG, NP)), dma((NG, NP)),
            dma((NG, NP)), dma((NG, NP)), dma((NG, NP)), dma((NG, NP)),
            dma((2, 2)), dma((2, 2)), dma((3, NP)), dma((3, NP)), dma((2,)),
        ],
        compiler_params=pltpu.CompilerParams(
            collective_id=0, has_side_effects=True, vmem_limit_bytes=48 << 20
        ),
        cost_estimate=pl.CostEstimate(flops=100_000_000, bytes_accessed=6 << 20, transcendentals=0),
        name="ice_subcycles",
    )(ocean_map[None], ice_map[None], ocean_state, land_mask, ice_motion, ice_mass, ice_strength, ice_mask)
    return pl.pallas_call(
        to_slots,
        out_shape=back,
        in_specs=[smem, smem, hbm, hbm],
        out_specs=(hbm, hbm),
        scratch_shapes=[dma((NP,)), dma((NP,))],
        name="to_slots",
    )(ocean_map, ice_map, ice_back, ocean_back)


def solution(mesh):
    blocks = P(("gx", "gy"), None, None, None)
    layer = P(("gx", "gy"), None, None)
    slots = P(("gx", "gy"))
    return jax.shard_map(
        shards, mesh=mesh,
        in_specs=(blocks, layer, slots, blocks, layer, layer, layer, slots),
        out_specs=(blocks, blocks), check_vma=False,
    )
```

```python
import functools

import jax
import jax.numpy as jnp
from jax import lax
from jax.experimental import pallas as pl
from jax.experimental.pallas import tpu as pltpu
from jax.sharding import PartitionSpec as P

BH = 32
BW = 128
NP = 16
NX = 8
ITERS = 8
DEEP = 16
HIGH = BH + 2 * DEEP
NBLK = NP + 1
EDGE = 8
ROWS = HIGH + 2 * EDGE
MESH = pl.DeviceIdType.MESH
F32 = jnp.float32

GROUPS = (
    (("u", "i"), ("v", "i"), ("p", "i")),
    (("s1", "i"), ("s2", "i"), ("s12", "i")),
    (("m", "i"), ("uo", "o"), ("vo", "o")),
    (("tx", "o"), ("ty", "o"), ("ac", "o")),
)
NG = len(GROUPS)
PER = 3
SIDE_SETS = (("u", "v", "p", "s1", "s2", "s12"), ("m", "uo", "vo", "tx", "ty", "ac"))
TILE_FIELDS = ("u", "v", "p", "s1", "s2", "s12", "m", "uo", "vo", "tx", "ty", "ac", "sa", "sc")


def shifted(col, k, sign):
    dx, dz = lax.div(k, 4), lax.rem(k, 4)
    x, z = lax.div(col, 4), lax.rem(col, 4)
    return lax.rem(x + sign * dx + 4, 4) * 4 + lax.rem(z + sign * dz + 4, 4)


def tile_col(block_id):
    return lax.rem(lax.div(block_id, NP), NP)


def x_difference(ref, off, j, lane):
    sl = pl.ds(EDGE + off, 8)
    here = ref[j, sl]
    up = pltpu.roll(jnp.where(lane == 0, ref[(j + 1) % NBLK, sl], here), BW - 1, 1)
    down = pltpu.roll(jnp.where(lane == BW - 1, ref[(j - 1) % NBLK, sl], here), 1, 1)
    return up - down


def y_difference(ref, off, j):
    return ref[j, pl.ds(EDGE + off + 1, 8)] - ref[j, pl.ds(EDGE + off - 1, 8)]


def stress_rows(t, off, j, lane):
    sl = pl.ds(EDGE + off, 8)
    east = x_difference(t["u"], off, j, lane)
    north = y_difference(t["v"], off, j)
    shear = y_difference(t["u"], off, j) + x_difference(t["v"], off, j, lane)
    diverg = east + north
    tension = east - north
    square = diverg * diverg + (tension * tension + shear * shear) * 0.25 + 0.16
    p = t["p"][j, sl]
    ratio = p * lax.rsqrt(square)
    s1 = 0.4 * t["s1"][j, sl] + (ratio * diverg - p)
    s2 = 0.4 * t["s2"][j, sl] + ratio * tension
    s12 = 0.4 * t["s12"][j, sl] + ratio * shear
    quarter = 0.25 * s2
    t["s1"][j, sl] = s1
    t["s2"][j, sl] = s2
    t["s12"][j, sl] = s12
    t["sa"][j, sl] = s1 + quarter
    t["sc"][j, sl] = s1 - quarter


def momentum_rows(t, off, j, lane):
    sl = pl.ds(EDGE + off, 8)
    force_x = x_difference(t["sa"], off, j, lane) * 0.25 + y_difference(t["s12"], off, j) * 0.0625
    force_y = x_difference(t["s12"], off, j, lane) * 0.0625 + y_difference(t["sc"], off, j) * 0.25
    u, v, m = t["u"][j, sl], t["v"][j, sl], t["m"][j, sl]
    uo, vo = t["uo"][j, sl], t["vo"][j, sl]
    diff_x, diff_y = uo - u, vo - v
    square = diff_x * diff_x + diff_y * diff_y + 0.01
    drag = square * lax.rsqrt(square)
    diag = m + drag
    rotate = 0.5 * m
    rhs_x = m * (u - t["tx"][j, sl]) + force_x + drag * uo
    rhs_y = m * (v - t["ty"][j, sl]) + force_y + drag * vo
    scale = t["ac"][j, sl] * pltpu.reciprocal(diag * diag + rotate * rotate, approx=True)
    t["u"][j, sl] = (diag * rhs_x + rotate * rhs_y) * scale
    t["v"][j, sl] = (diag * rhs_y - rotate * rhs_x) * scale


def body(
    omap_h, imap_h, ocean_h, land_h, motion_h, mass_h, strength_h, mask_h,
    ice_out, ocean_out,
    omap, imap, ocean, land, motion, mass, strength, mask,
    send, recv, top, bottom, ids_send, ids_recv, ids_top, ids_bottom, order_v, inverse_v,
    order, inverse, side_send, side_recv, back_ice, back_ocean, tile,
    in_sem, id_s, id_r, idf_s, idf_r, small_sem, data_s, data_r,
    top_s, top_r, bot_s, bot_r, side_s, side_r, back_s, back_r, own_sem,
):
    gx, gy = lax.axis_index("gx"), lax.axis_index("gy")
    t = dict(zip(TILE_FIELDS, tile))
    lane = lax.broadcasted_iota(jnp.int32, (8, BW), 1)
    row8 = lax.broadcasted_iota(jnp.int32, (8, BW), 0)

    barrier = pltpu.get_barrier_semaphore()

    def greet(k, _):
        pl.semaphore_signal(barrier, inc=1, device_id=(gx, shifted(gy, k, 1)), device_id_type=MESH)
        return 0

    lax.fori_loop(1, NP, greet, 0)
    for d in (1, NX - 1):
        pl.semaphore_signal(
            barrier, inc=1, device_id=(lax.rem(gx + d, NX), gy), device_id_type=MESH
        )
    map_loads = [
        pltpu.make_async_copy(imap_h, imap, in_sem.at[6]),
        pltpu.make_async_copy(omap_h, omap, in_sem.at[7]),
    ]
    loads = [
        pltpu.make_async_copy(motion_h, motion, in_sem.at[0]),
        pltpu.make_async_copy(strength_h, strength, in_sem.at[1]),
        pltpu.make_async_copy(mass_h, mass, in_sem.at[2]),
        pltpu.make_async_copy(mask_h, mask, in_sem.at[3]),
        pltpu.make_async_copy(ocean_h, ocean, in_sem.at[4]),
        pltpu.make_async_copy(land_h, land, in_sem.at[5]),
    ]
    for load in map_loads + loads:
        load.start()
    for load in map_loads:
        load.wait()

    tile_of = lax.broadcasted_iota(jnp.int32, (NP, NP), 0)
    slot_of = lax.broadcasted_iota(jnp.int32, (NP, NP), 1)
    places = []
    for row, blocks in ((0, imap), (1, omap)):
        block = jnp.broadcast_to(blocks[...], (NP, NP))
        same = tile_col(block) == tile_of
        slot = jnp.max(jnp.where(same, slot_of, 0), axis=1, keepdims=True)
        place_in = jnp.max(jnp.where(same, lax.rem(block, NP), 0), axis=1, keepdims=True)
        order_v[row] = jnp.broadcast_to(slot, (NP, BW))
        places.append(jnp.broadcast_to(place_in, (NP, BW)))
    order_copy = pltpu.make_async_copy(order_v, order, small_sem.at[0])
    order_copy.start()
    for c in range(NP):
        ids_send[c] = jnp.where(row8 == 0, places[0][c : c + 1], places[1][c : c + 1])
    ids_recv[0] = ids_send[gy]
    order_copy.wait()

    def packed(name, si, so):
        if name == "p":
            return strength[si] * 0.3
        if name == "m":
            return mass[si] * mask[si].astype(F32)
        if name == "ac":
            return (1 - land[so]).astype(F32)
        if name in ("u", "v", "s1"):
            return motion[si, ("u", "v", "s1").index(name)]
        if name == "s2":
            return motion[si, 3] * 4.0
        if name == "s12":
            return motion[si, 4] * 8.0
        return ocean[so, ("uo", "vo", "tx", "ty").index(name)]

    def pack(g):
        def one(k, _):
            c = shifted(gy, k, 1)
            si, so = order[0, c, 0], order[1, c, 0]
            for f, (name, _kind) in enumerate(GROUPS[g]):
                send[g, k, f] = packed(name, si, so)
            return 0

        lax.fori_loop(1, NP, one, 0)
        si, so = order[0, gy, 0], order[1, gy, 0]
        for f, (name, _kind) in enumerate(GROUPS[g]):
            recv[g][0, f] = packed(name, si, so)

    def data_copy(g, k):
        return pltpu.make_async_remote_copy(
            src_ref=send.at[g, k], dst_ref=recv[g].at[k],
            send_sem=data_s.at[g, k], recv_sem=data_r.at[g, k],
            device_id=(gx, shifted(gy, k, 1)), device_id_type=MESH,
        )

    def id_copy(k):
        return pltpu.make_async_remote_copy(
            src_ref=ids_send.at[shifted(gy, k, 1)], dst_ref=ids_recv.at[k],
            send_sem=id_s.at[k], recv_sem=id_r.at[k],
            device_id=(gx, shifted(gy, k, 1)), device_id_type=MESH,
        )

    def top_copy(g, k):
        return pltpu.make_async_remote_copy(
            src_ref=recv[g].at[k, :, pl.ds(DEEP, DEEP)], dst_ref=top[g].at[k],
            send_sem=top_s.at[g, k], recv_sem=top_r.at[g, k],
            device_id=(gx + 1, gy), device_id_type=MESH,
        )

    def bottom_copy(g, k):
        return pltpu.make_async_remote_copy(
            src_ref=recv[g].at[k, :, pl.ds(0, DEEP)], dst_ref=bottom[g].at[k],
            send_sem=bot_s.at[g, k], recv_sem=bot_r.at[g, k],
            device_id=(gx - 1, gy), device_id_type=MESH,
        )

    def id_forward(d):
        return pltpu.make_async_remote_copy(
            src_ref=ids_recv, dst_ref=(ids_top, ids_bottom)[d],
            send_sem=idf_s.at[d], recv_sem=idf_r.at[d],
            device_id=((gx + 1, gx - 1)[d], gy), device_id_type=MESH,
        )

    def each(lo, fn):
        def step(k, _):
            fn(k)
            return 0

        lax.fori_loop(lo, NP, step, 0)

    loads[0].wait()
    loads[1].wait()
    pack(0)
    pl.semaphore_wait(barrier, NP - 1 + 2)
    each(1, lambda k: id_copy(k).start())
    each(1, lambda k: data_copy(0, k).start())
    pack(1)
    each(1, lambda k: data_copy(1, k).start())
    for load in loads[2:5]:
        load.wait()
    pack(2)
    each(1, lambda k: data_copy(2, k).start())
    loads[5].wait()
    pack(3)
    each(1, lambda k: data_copy(3, k).start())

    @pl.when(gx == 0)
    def _():
        ids_top[...] = jnp.zeros(ids_top.shape, jnp.int32)

        def clear(k):
            for g in range(NG):
                top[g][k] = jnp.zeros((PER, DEEP, BW), F32)

        each(0, clear)

    @pl.when(gx == NX - 1)
    def _():
        ids_bottom[...] = jnp.zeros(ids_bottom.shape, jnp.int32)

        def clear(k):
            for g in range(NG):
                bottom[g][k] = jnp.zeros((PER, DEEP, BW), F32)

        each(0, clear)

    for e in range(2):

        @pl.when(gy == (0, NP - 1)[e])
        def _():
            side_recv[:, e] = jnp.zeros((2, HIGH, BW), F32)

    for name in TILE_FIELDS:
        t[name][:, pl.ds(0, EDGE)] = jnp.zeros((NBLK, EDGE, BW), F32)
        t[name][:, pl.ds(ROWS - EDGE, EDGE)] = jnp.zeros((NBLK, EDGE, BW), F32)

    each(1, lambda k: id_copy(k).wait_recv())

    @pl.when(gx < NX - 1)
    def _():
        id_forward(0).start()

    @pl.when(gx > 0)
    def _():
        id_forward(1).start()

    def invert(which, source):
        found = jnp.zeros((8, BW), jnp.int32)
        for k in range(NP):
            found = jnp.maximum(found, jnp.where(source[k] == lane, k, 0))
        inverse_v[which] = found
        copy = pltpu.make_async_copy(inverse_v.at[which], inverse.at[which], small_sem.at[1 + which])
        copy.start()
        copy.wait()

    invert(0, ids_recv)
    place_of = jnp.zeros((8, BW), jnp.int32)
    for k in range(NP):
        place_of = jnp.where(lane == k, ids_recv[k], place_of)
    inverse_v[3] = place_of
    place_copy = pltpu.make_async_copy(inverse_v.at[3], inverse.at[3], small_sem.at[4])
    place_copy.start()
    place_copy.wait()

    @pl.when(gx > 0)
    def _():
        id_forward(0).wait_recv()

    invert(1, ids_top)

    @pl.when(gx < NX - 1)
    def _():
        id_forward(1).wait_recv()

    invert(2, ids_bottom)

    def forward(g, k):
        @pl.when(gx < NX - 1)
        def _():
            top_copy(g, k).start()

        @pl.when(gx > 0)
        def _():
            bottom_copy(g, k).start()

    def place(g, which, source, row, rows):
        def one(j):
            for f, (name, kind) in enumerate(GROUPS[g]):
                src = inverse[which, "io".index(kind), j]
                sl = pl.ds(EDGE + row, rows)
                value = source[src, f]
                if name == "ac":
                    value = jnp.where(t["m"][j, sl] > 0.0, value, 0.0)
                t[name][j, sl] = value

        each(0, one)

    def place_halo(g):
        @pl.when(gx > 0)
        def _():
            each(0, lambda k: top_copy(g, k).wait_recv())

        @pl.when(gx < NX - 1)
        def _():
            each(0, lambda k: bottom_copy(g, k).wait_recv())

        place(g, 1, top[g], 0, DEEP)
        place(g, 2, bottom[g], DEEP + BH, DEEP)

    def side_copy(n, e):
        return pltpu.make_async_remote_copy(
            src_ref=side_send.at[n, e], dst_ref=side_recv.at[n, e],
            send_sem=side_s.at[n, e], recv_sem=side_r.at[n, e],
            device_id=(gx, (gy + 1, gy - 1)[e]), device_id_type=MESH,
        )

    def send_sides(n):
        for a in range(HIGH // 8):
            right = jnp.zeros((8, BW), F32)
            left = jnp.zeros((8, BW), F32)
            for f, name in enumerate(SIDE_SETS[n]):
                here = (lane >= DEEP * f) & (lane < DEEP * (f + 1))
                r = t[name][NP - 1, pl.ds(EDGE + 8 * a, 8)]
                q = t[name][0, pl.ds(EDGE + 8 * a, 8)]
                right = jnp.where(here, pltpu.roll(r, (DEEP * f + DEEP) % BW, 1), right)
                left = jnp.where(here, pltpu.roll(q, DEEP * f, 1) if f else q, left)
            side_send[n, 0, pl.ds(8 * a, 8)] = right
            side_send[n, 1, pl.ds(8 * a, 8)] = left

        @pl.when(gy < NP - 1)
        def _():
            side_copy(n, 0).start()

        @pl.when(gy > 0)
        def _():
            side_copy(n, 1).start()

    def take_sides(n):
        @pl.when(gy > 0)
        def _():
            side_copy(n, 0).wait_recv()

        @pl.when(gy < NP - 1)
        def _():
            side_copy(n, 1).wait_recv()

        for a in range(HIGH // 8):
            left = side_recv[n, 0, pl.ds(8 * a, 8)]
            right = side_recv[n, 1, pl.ds(8 * a, 8)]
            for f, name in enumerate(SIDE_SETS[n]):
                r = pltpu.roll(right, BW - DEEP * f, 1) if f else right
                q = pltpu.roll(left, BW - DEEP - DEEP * f, 1)
                value = jnp.where(lane < DEEP, r, jnp.where(lane >= BW - DEEP, q, 0.0))
                t[name][NP, pl.ds(EDGE + 8 * a, 8)] = value

    def arrive(g):
        def one(k):
            data_copy(g, k).wait_recv()
            forward(g, k)

        forward(g, 0)
        each(1, one)
        place(g, 0, recv[g], DEEP, BH)

    arrive(0)
    arrive(1)
    place_halo(0)
    arrive(2)
    place_halo(1)
    send_sides(0)
    arrive(3)
    place_halo(2)
    place_halo(3)
    send_sides(1)
    take_sides(0)
    take_sides(1)

    def subcycle(n, _):
        skip_s, skip_m = lax.div(n, 4), lax.div(n + 1, 4)

        def stress_step(i, _):
            for a in range(2):
                off = (skip_s + 2 * i + a) * 8
                for j in range(NBLK):
                    stress_rows(t, off, j, lane)
            return 0

        lax.fori_loop(0, 4 - skip_s, stress_step, 0)

        def momentum_step(i, _):
            for a in range(2):
                off = (skip_m + 2 * i + a) * 8
                for j in range(NBLK):
                    momentum_rows(t, off, j, lane)
            return 0

        lax.fori_loop(0, 4 - skip_m, momentum_step, 0)
        return 0

    lax.fori_loop(0, ITERS, subcycle, 0)

    def back_copy(part, k):
        src, dst = (
            (back_ice.at[k, pl.ds(2, 3)], ice_out.at[k, pl.ds(2, 3)]),
            (back_ice.at[k, pl.ds(0, 2)], ice_out.at[k, pl.ds(0, 2)]),
            (back_ocean.at[k], ocean_out.at[k]),
        )[part]
        return pltpu.make_async_remote_copy(
            src_ref=src, dst_ref=dst, send_sem=back_s.at[part, k], recv_sem=back_r.at[part, k],
            device_id=(gx, shifted(gy, k, -1)), device_id_type=MESH,
        )

    def mine(name, at):
        return t[name][at, pl.ds(EDGE + DEEP, BH)]

    def pack_stress(k):
        at = inverse[3, 0, k]
        back_ice[k, 2] = mine("s1", at)
        back_ice[k, 3] = mine("s2", at) * 0.25
        back_ice[k, 4] = mine("s12", at) * 0.125

    def pack_velocity(k):
        at = inverse[3, 0, k]
        back_ice[k, 0] = mine("u", at)
        back_ice[k, 1] = mine("v", at)

    def pack_ocean(k):
        at = inverse[3, 1, k]
        diff_x = mine("u", at) - mine("uo", at)
        diff_y = mine("v", at) - mine("vo", at)
        square = diff_x * diff_x + diff_y * diff_y + 0.01
        drag = mine("ac", at) * (square * lax.rsqrt(square))
        back_ocean[k, 0] = drag * diff_x
        back_ocean[k, 1] = drag * diff_y

    def give_back(part, fill):
        def one(k):
            fill(k)
            back_copy(part, k).start()

        each(1, one)
        fill(0)

    give_back(0, pack_stress)
    give_back(1, pack_velocity)
    give_back(2, pack_ocean)
    own_ice = pltpu.make_async_copy(back_ice.at[0], ice_out.at[0], own_sem.at[0])
    own_ocean = pltpu.make_async_copy(back_ocean.at[0], ocean_out.at[0], own_sem.at[1])
    own_ice.start()
    own_ocean.start()

    def drain(k):
        id_copy(k).wait_send()
        for g in range(NG):
            data_copy(g, k).wait_send()

    each(1, drain)

    @pl.when(gx < NX - 1)
    def _():
        id_forward(0).wait_send()

        def one(k):
            for g in range(NG):
                top_copy(g, k).wait_send()

        each(0, one)

    @pl.when(gx > 0)
    def _():
        id_forward(1).wait_send()

        def one(k):
            for g in range(NG):
                bottom_copy(g, k).wait_send()

        each(0, one)

    @pl.when(gy < NP - 1)
    def _():
        for n in range(2):
            side_copy(n, 0).wait_send()

    @pl.when(gy > 0)
    def _():
        for n in range(2):
            side_copy(n, 1).wait_send()

    own_ice.wait()
    own_ocean.wait()

    def finish(k):
        for part in range(3):
            back_copy(part, k).wait_recv()

    each(1, finish)

    def finish_send(k):
        for part in range(3):
            back_copy(part, k).wait_send()

    each(1, finish_send)


def to_slots(omap, imap, ice, ocean, ice_out, ocean_out, sem):
    gy = lax.axis_index("gy")
    x, z = lax.div(gy, 4), lax.rem(gy, 4)
    copies = []
    for n, (blocks, held, out) in enumerate(((imap, ice, ice_out), (omap, ocean, ocean_out))):
        for s in range(NP):
            c = tile_col(blocks[s])
            cx, cz = lax.div(c, 4), lax.rem(c, 4)
            k = lax.rem(cx - x + 4, 4) * 4 + lax.rem(cz - z + 4, 4)
            copies.append(pltpu.make_async_copy(held.at[k], out.at[s], sem.at[n, s]))
            copies[-1].start()
    for copy in copies:
        copy.wait()


def shards(ocean_state, land_mask, ocean_map, ice_motion, ice_mass, ice_strength, ice_mask, ice_map):
    dma = pltpu.SemaphoreType.DMA
    vmem = pltpu.VMEM
    hbm = pl.BlockSpec(memory_space=pltpu.HBM)
    smem = pl.BlockSpec(memory_space=pltpu.SMEM)
    held = pl.BlockSpec(memory_space=pltpu.VMEM)
    back = (
        jax.ShapeDtypeStruct((NP, 5, BH, BW), F32),
        jax.ShapeDtypeStruct((NP, 2, BH, BW), F32),
    )
    ids = vmem((NP, 8, BW), jnp.int32)
    ice_back, ocean_back = pl.pallas_call(
        body,
        out_shape=back,
        in_specs=[hbm] * 8,
        out_specs=(hbm, hbm),
        scratch_shapes=[
            vmem((1, NP), jnp.int32),
            vmem((1, NP), jnp.int32),
            vmem((NP, 4, BH, BW), F32),
            vmem((NP, BH, BW), jnp.int32),
            vmem((NP, 5, BH, BW), F32),
            vmem((NP, BH, BW), F32),
            vmem((NP, BH, BW), F32),
            vmem((NP, BH, BW), jnp.int32),
            vmem((NG, NP, PER, BH, BW), F32),
            [vmem((NP, PER, BH, BW), F32) for _ in GROUPS],
            [vmem((NP, PER, DEEP, BW), F32) for _ in GROUPS],
            [vmem((NP, PER, DEEP, BW), F32) for _ in GROUPS],
            ids, ids, ids, ids,
            vmem((2, NP, BW), jnp.int32),
            vmem((4, 8, BW), jnp.int32),
            pltpu.SMEM((2, NP, BW), jnp.int32),
            pltpu.SMEM((4, 8, BW), jnp.int32),
            vmem((2, 2, HIGH, BW), F32),
            vmem((2, 2, HIGH, BW), F32),
            vmem((NP, 5, BH, BW), F32),
            vmem((NP, 2, BH, BW), F32),
            [vmem((NBLK, ROWS, BW), F32) for _ in TILE_FIELDS],
            dma((8,)), dma((NP,)), dma((NP,)), dma((2,)), dma((2,)), dma((5,)),
            dma((NG, NP)), dma((NG, NP)),
            dma((NG, NP)), dma((NG, NP)), dma((NG, NP)), dma((NG, NP)),
            dma((2, 2)), dma((2, 2)), dma((3, NP)), dma((3, NP)), dma((2,)),
        ],
        compiler_params=pltpu.CompilerParams(
            collective_id=0, has_side_effects=True, vmem_limit_bytes=48 << 20
        ),
        cost_estimate=pl.CostEstimate(flops=100_000_000, bytes_accessed=6 << 20, transcendentals=0),
        name="ice_subcycles",
    )(*[
        pltpu.with_memory_space_constraint(array, pltpu.HBM)
        for array in (
            ocean_map[None], ice_map[None], ocean_state, land_mask,
            ice_motion, ice_mass, ice_strength, ice_mask,
        )
    ])
    return pl.pallas_call(
        to_slots,
        out_shape=back,
        in_specs=[smem, smem, held, held],
        out_specs=(hbm, hbm),
        scratch_shapes=[
            dma((2, NP)),
        ],
        compiler_params=pltpu.CompilerParams(vmem_limit_bytes=16 << 20),
        name="to_slots",
    )(ocean_map, ice_map, ice_back, ocean_back)


def solution(mesh):
    blocks = P(("gx", "gy"), None, None, None)
    layer = P(("gx", "gy"), None, None)
    slots = P(("gx", "gy"))
    return jax.shard_map(
        shards, mesh=mesh,
        in_specs=(blocks, layer, slots, blocks, layer, layer, layer, slots),
        out_specs=(blocks, blocks), check_vma=False,
    )
```

```python
import functools

import jax
import jax.numpy as jnp
from jax import lax
from jax.experimental import pallas as pl
from jax.experimental.pallas import tpu as pltpu
from jax.sharding import PartitionSpec as P

BH = 32
BW = 128
NP = 16
NX = 8
ITERS = 8
DEEP = 16
HIGH = BH + 2 * DEEP
EDGE = 24
CHUNK = 8
NC = BH // CHUNK
ROWS = HIGH + 2 * EDGE
MESH = pl.DeviceIdType.MESH
F32 = jnp.float32

ICE = ("u", "v", "p", "s1", "s2", "s12", "m")
OCEAN = ("uo", "vo", "tx", "ty", "ac")
FIELDS = ICE + OCEAN
NF = len(FIELDS)
SIDE_SETS = (FIELDS[:6], FIELDS[6:])
TILE_FIELDS = FIELDS + ("sa", "sc")
RESULTS = 7
OWN_ROW = (16, 24, 32, 40)
HALO_ROW = (8, 0, 56, 48)
SIDE_ROW = (16, 8, 24, 0, 32, 40, 48, 56)
SIDE_OWN = (0, 2, 4, 5)
SIDE_HALO = (1, 3, 7, 6)
NS = len(SIDE_ROW)


def shifted(col, k, sign):
    dx, dz = lax.div(k, 4), lax.rem(k, 4)
    x, z = lax.div(col, 4), lax.rem(col, 4)
    return lax.rem(x + sign * dx + 4, 4) * 4 + lax.rem(z + sign * dz + 4, 4)


def tile_col(block_id):
    return lax.rem(lax.div(block_id, NP), NP)


def x_difference(ref, off, j, lane):
    sl = pl.ds(EDGE + off, 8)
    here = ref[j, sl]
    if not isinstance(j, int):
        return pltpu.roll(here, BW - 1, 1) - pltpu.roll(here, 1, 1)
    up = pltpu.roll(jnp.where(lane == 0, ref[(j + 1) % NP, sl], here), BW - 1, 1)
    down = pltpu.roll(jnp.where(lane == BW - 1, ref[(j - 1) % NP, sl], here), 1, 1)
    return up - down


def y_difference(ref, off, j):
    return ref[j, pl.ds(EDGE + off + 1, 8)] - ref[j, pl.ds(EDGE + off - 1, 8)]


def stress_rows(t, off, j, lane):
    sl = pl.ds(EDGE + off, 8)
    east = x_difference(t["u"], off, j, lane)
    north = y_difference(t["v"], off, j)
    shear = y_difference(t["u"], off, j) + x_difference(t["v"], off, j, lane)
    diverg = east + north
    tension = east - north
    square = diverg * diverg + (tension * tension + shear * shear) * 0.25 + 0.16
    p = t["p"][j, sl]
    ratio = p * lax.rsqrt(square)
    s1 = 0.4 * t["s1"][j, sl] + (ratio * diverg - p)
    s2 = 0.4 * t["s2"][j, sl] + ratio * tension
    s12 = 0.4 * t["s12"][j, sl] + ratio * shear
    quarter = 0.25 * s2
    t["s1"][j, sl] = s1
    t["s2"][j, sl] = s2
    t["s12"][j, sl] = s12
    t["sa"][j, sl] = s1 + quarter
    t["sc"][j, sl] = s1 - quarter


def momentum_rows(t, off, j, lane):
    sl = pl.ds(EDGE + off, 8)
    force_x = x_difference(t["sa"], off, j, lane) * 0.25 + y_difference(t["s12"], off, j) * 0.0625
    force_y = x_difference(t["s12"], off, j, lane) * 0.0625 + y_difference(t["sc"], off, j) * 0.25
    u, v, m = t["u"][j, sl], t["v"][j, sl], t["m"][j, sl]
    uo, vo = t["uo"][j, sl], t["vo"][j, sl]
    diff_x, diff_y = uo - u, vo - v
    square = diff_x * diff_x + diff_y * diff_y + 0.01
    drag = square * lax.rsqrt(square)
    diag = m + drag
    rotate = 0.5 * m
    rhs_x = m * (u - t["tx"][j, sl]) + force_x + drag * uo
    rhs_y = m * (v - t["ty"][j, sl]) + force_y + drag * vo
    scale = t["ac"][j, sl] * pltpu.reciprocal(diag * diag + rotate * rotate, approx=True)
    t["u"][j, sl] = (diag * rhs_x + rotate * rhs_y) * scale
    t["v"][j, sl] = (diag * rhs_y - rotate * rhs_x) * scale


def body(
    omap_h, imap_h, ocean_h, land_h, motion_h, mass_h, strength_h, mask_h,
    out,
    omap, imap, ocean, land, motion, mass, strength, mask,
    send, recv, halo, ids_send, ids_recv, ids_up, ids_low, order_v, inverse_v,
    order, inverse, side_send, side_recv, back, tile, strip,
    in_sem, map_sem, id_s, id_r, idf_s, idf_r, small_sem, data_s, data_r,
    halo_s, halo_r, side_s, side_r, back_s, back_r, own_sem,
):
    gx, gy = lax.axis_index("gx"), lax.axis_index("gy")
    odd = lax.rem(gx, 2)
    sign = 1 - 2 * odd
    up, low = gx - sign, gx + sign
    has_up = (gx > 0) & (gx < NX - 1)
    t = dict(zip(TILE_FIELDS, tile))
    edge = dict(zip(TILE_FIELDS, strip))
    lane = lax.broadcasted_iota(jnp.int32, (8, BW), 1)
    row8 = lax.broadcasted_iota(jnp.int32, (8, BW), 0)

    def actual(row):
        return odd * (HIGH - 8) + sign * row

    def chunk_at(i):
        return odd * (BH - CHUNK) + sign * (CHUNK * i)

    barrier = pltpu.get_barrier_semaphore()

    def greet(k, _):
        pl.semaphore_signal(barrier, inc=1, device_id=(gx, shifted(gy, k, 1)), device_id_type=MESH)
        return 0

    lax.fori_loop(1, NP, greet, 0)
    for d in (1, NX - 1):
        pl.semaphore_signal(
            barrier, inc=1, device_id=(lax.rem(gx + d, NX), gy), device_id_type=MESH
        )
    map_loads = [
        pltpu.make_async_copy(imap_h, imap, map_sem.at[0]),
        pltpu.make_async_copy(omap_h, omap, map_sem.at[1]),
    ]
    loads = []
    for i in range(NC):
        rows = pl.ds(chunk_at(i), CHUNK)
        loads.append([
            pltpu.make_async_copy(motion_h.at[:, :, rows], motion[i], in_sem.at[i, 0]),
            pltpu.make_async_copy(strength_h.at[:, rows], strength[i], in_sem.at[i, 1]),
            pltpu.make_async_copy(mass_h.at[:, rows], mass[i], in_sem.at[i, 2]),
            pltpu.make_async_copy(mask_h.at[:, rows], mask[i], in_sem.at[i, 3]),
            pltpu.make_async_copy(ocean_h.at[:, :, rows], ocean[i], in_sem.at[i, 4]),
            pltpu.make_async_copy(land_h.at[:, rows], land[i], in_sem.at[i, 5]),
        ])
    for load in map_loads + sum(loads, []):
        load.start()
    for load in map_loads:
        load.wait()

    tile_of = lax.broadcasted_iota(jnp.int32, (NP, NP), 0)
    slot_of = lax.broadcasted_iota(jnp.int32, (NP, NP), 1)
    places = []
    found = jnp.zeros((8, BW), jnp.int32)
    lane16 = lax.broadcasted_iota(jnp.int32, (NP, BW), 1)
    row16 = lax.broadcasted_iota(jnp.int32, (NP, BW), 0)
    for row, blocks in ((0, imap), (1, omap)):
        block = jnp.broadcast_to(blocks[...], (NP, NP))
        same = tile_col(block) == tile_of
        slot = jnp.max(jnp.where(same, slot_of, 0), axis=1, keepdims=True)
        place_in = jnp.max(jnp.where(same, lax.rem(block, NP), 0), axis=1, keepdims=True)
        slot = jnp.broadcast_to(slot, (NP, BW))
        slot = jnp.max(jnp.where(lane16 == row16, slot, 0), axis=0, keepdims=True)
        found = jnp.where(row8 == row, slot, found)
        places.append(jnp.broadcast_to(place_in, (NP, BW)))
    order_v[...] = found
    order_copy = pltpu.make_async_copy(order_v, order, small_sem.at[0])
    order_copy.start()
    for c in range(NP):
        ids_send[c] = jnp.where(row8 == 0, places[0][c : c + 1], places[1][c : c + 1])
    ids_recv[0] = ids_send[gy]
    order_copy.wait()

    def packed(i, name, si, so):
        if name == "p":
            return strength[i][si] * 0.3
        if name == "m":
            return mass[i][si] * mask[i][si].astype(F32)
        if name == "ac":
            return (1 - land[i][so]).astype(F32)
        if name in ("u", "v", "s1"):
            return motion[i][si, ("u", "v", "s1").index(name)]
        if name == "s2":
            return motion[i][si, 3] * 4.0
        if name == "s12":
            return motion[i][si, 4] * 8.0
        return ocean[i][so, ("uo", "vo", "tx", "ty").index(name)]

    def each(lo, fn, hi=NP, unroll=None):
        def step(k, _):
            fn(k)
            return 0

        lax.fori_loop(lo, hi, step, 0, unroll=unroll)

    def pack(i):
        def one(k):
            c = shifted(gy, k, 1)
            si, so = order[0, c], order[1, c]
            for f, name in enumerate(FIELDS):
                send[i, k, f] = packed(i, name, si, so)

        each(1, one, unroll=5)
        si, so = order[0, gy], order[1, gy]
        for f, name in enumerate(FIELDS):
            recv[i][0, f] = packed(i, name, si, so)

    def data_copy(i, k):
        return pltpu.make_async_remote_copy(
            src_ref=send.at[i, k], dst_ref=recv[i].at[k],
            send_sem=data_s.at[i, k], recv_sem=data_r.at[i, k],
            device_id=(gx, shifted(gy, k, 1)), device_id_type=MESH,
        )

    def id_copy(k):
        return pltpu.make_async_remote_copy(
            src_ref=ids_send.at[shifted(gy, k, 1)], dst_ref=ids_recv.at[k],
            send_sem=id_s.at[k], recv_sem=id_r.at[k],
            device_id=(gx, shifted(gy, k, 1)), device_id_type=MESH,
        )

    def halo_copy(i, k):
        return pltpu.make_async_remote_copy(
            src_ref=recv[i].at[k], dst_ref=halo[i].at[k],
            send_sem=halo_s.at[i, k], recv_sem=halo_r.at[i, k],
            device_id=(up if i < 2 else low, gy), device_id_type=MESH,
        )

    def id_forward(d):
        return pltpu.make_async_remote_copy(
            src_ref=ids_recv, dst_ref=(ids_up, ids_low)[d],
            send_sem=idf_s.at[d], recv_sem=idf_r.at[d],
            device_id=((up, low)[d], gy), device_id_type=MESH,
        )

    for i in range(NC):
        for load in loads[i]:
            load.wait()
        pack(i)
        if i == 0:
            pl.semaphore_wait(barrier, NP - 1 + 2)
            each(1, lambda k: id_copy(k).start())
        each(1, lambda k: data_copy(i, k).start())

    @pl.when(jnp.logical_not(has_up))
    def _():
        for name in FIELDS:
            t[name][:, pl.ds(EDGE + odd * (HIGH - DEEP), DEEP)] = jnp.zeros((NP, DEEP, BW), F32)

    for e in range(2):

        @pl.when(gy == (0, NP - 1)[e])
        def _():
            side_recv[:, e] = jnp.zeros((NS, 2, 8, BW), F32)

    each(1, lambda k: id_copy(k).wait_recv())

    @pl.when(has_up)
    def _():
        id_forward(0).start()

    id_forward(1).start()

    def invert(which, source):
        found = jnp.zeros((8, BW), jnp.int32)
        for k in range(NP):
            found = jnp.maximum(found, jnp.where(source[k] == lane, k, 0))
        inverse_v[which] = found
        copy = pltpu.make_async_copy(
            inverse_v.at[which], inverse.at[which], small_sem.at[1 + which]
        )
        copy.start()
        copy.wait()

    invert(0, ids_recv)
    place_of = jnp.zeros((8, BW), jnp.int32)
    for k in range(NP):
        place_of = jnp.where(lane == k, ids_recv[k], place_of)
    inverse_v[3] = place_of
    place_copy = pltpu.make_async_copy(inverse_v.at[3], inverse.at[3], small_sem.at[4])
    place_copy.start()
    place_copy.wait()

    @pl.when(has_up)
    def _():
        id_forward(0).wait_recv()
        invert(1, ids_up)

    id_forward(1).wait_recv()
    invert(2, ids_low)

    def forward(i, k):
        if i < 2:

            @pl.when(has_up)
            def _():
                halo_copy(i, k).start()

        else:
            halo_copy(i, k).start()

    def arrive(i, lo, hi):
        def one(k):
            data_copy(i, k).wait_recv()
            forward(i, k)

        each(lo, one, hi)

    def place(which, source, row):
        sl = pl.ds(EDGE + row, CHUNK)

        def one(j):
            si, so = inverse[which, 0, j], inverse[which, 1, j]
            for f, name in enumerate(FIELDS):
                value = source[si if name in ICE else so, f]
                if name == "ac":
                    value = jnp.where(source[si, FIELDS.index("m")] > 0.0, value, 0.0)
                t[name][j, sl] = value

        each(0, one, unroll=4)

    def place_halo(i):
        def take():
            each(0, lambda k: halo_copy(i, k).wait_recv())
            place(1 if i < 2 else 2, halo[i], actual(HALO_ROW[i]))

        if i < 2:
            pl.when(has_up)(take)
        else:
            take()

    def side_copy(m, e):
        return pltpu.make_async_remote_copy(
            src_ref=side_send.at[m, e], dst_ref=side_recv.at[m, e],
            send_sem=side_s.at[m, e], recv_sem=side_r.at[m, e],
            device_id=(gx, (gy + 1, gy - 1)[e]), device_id_type=MESH,
        )

    def send_sides(m):
        sl = pl.ds(EDGE + actual(SIDE_ROW[m]), CHUNK)
        for n, names in enumerate(SIDE_SETS):
            right = jnp.zeros((8, BW), F32)
            left = jnp.zeros((8, BW), F32)
            for f, name in enumerate(names):
                here = (lane >= DEEP * f) & (lane < DEEP * (f + 1))
                r = t[name][NP - 1, sl]
                q = t[name][0, sl]
                right = jnp.where(here, pltpu.roll(r, (DEEP * f + DEEP) % BW, 1), right)
                left = jnp.where(here, pltpu.roll(q, DEEP * f, 1) if f else q, left)
                first = jnp.where((lane >= 16) & (lane < 48), pltpu.roll(q, 16, 1), 0.0)
                last = pltpu.roll(r, BW - 32, 1)
                edge[name][0, sl] = jnp.where((lane >= 64) & (lane < 96), last, first)
            side_send[m, 0, n] = right
            side_send[m, 1, n] = left

        @pl.when(gy < NP - 1)
        def _():
            side_copy(m, 0).start()

        @pl.when(gy > 0)
        def _():
            side_copy(m, 1).start()

    def take_sides(m, row):
        @pl.when(gy > 0)
        def _():
            side_copy(m, 0).wait_recv()

        @pl.when(gy < NP - 1)
        def _():
            side_copy(m, 1).wait_recv()

        sl = pl.ds(EDGE + actual(row), CHUNK)
        for n, names in enumerate(SIDE_SETS):
            left = side_recv[m, 0, n]
            right = side_recv[m, 1, n]
            for f, name in enumerate(names):
                q = pltpu.roll(left, BW - DEEP * f, 1) if f else left
                r = pltpu.roll(right, 96 - DEEP * f, 1) if f < 6 else right
                value = jnp.where((lane >= 96) & (lane < 112), r, edge[name][0, sl])
                edge[name][0, sl] = jnp.where(lane < DEEP, q, value)

    def lowest(row, windows):
        return odd * (HIGH - 8) + sign * row - 8 * (windows - 1) * (1 - odd)

    def half_step(rows_of, row, windows=1, strip_row=None, strip_windows=1, strip_at=0):
        off = lowest(row, windows)
        for i in range(windows):
            for j in range(NP):
                rows_of(t, off + 8 * i, j, lane)
        if strip_row is not None:
            off = lowest(strip_row, strip_windows)
            for i in range(strip_windows):
                rows_of(edge, off + 8 * i, jnp.int32(strip_at), lane)

    def wave(end, beside, strip_end, strip_windows=1, strip_at=0):
        def one(n):
            h = 2 * n + 1
            half_step(stress_rows, end - h, 1, strip_end - h, strip_windows, strip_at)
            half_step(momentum_rows, end - h - 1, 1, strip_end - h - 1, strip_windows, strip_at)
            beside(n)

        each(0, one, ITERS)

    def first_waves(beside):
        def one(n):
            each(0, lambda i: half_step(stress_rows, 23 - 2 * n - 16 * i, 2), lax.div(45 - 4 * n, 16))
            each(0, lambda i: half_step(momentum_rows, 22 - 2 * n - 16 * i, 2), lax.div(43 - 4 * n, 16))
            beside(n)

        each(0, one, ITERS)

    def strip_wave(end, beside):
        def one(n):
            stress_rows(edge, actual(end - 2 * n - 1), jnp.int32(0), lane)
            momentum_rows(edge, actual(end - 2 * n - 2), jnp.int32(0), lane)
            beside(n)

        each(0, one, ITERS)

    def back_copy(i, k):
        return pltpu.make_async_remote_copy(
            src_ref=back.at[i, k], dst_ref=out.at[k, :, pl.ds(chunk_at(i), CHUNK)],
            send_sem=back_s.at[i, k], recv_sem=back_r.at[i, k],
            device_id=(gx, shifted(gy, k, -1)), device_id_type=MESH,
        )

    def own_copy(i):
        return pltpu.make_async_copy(
            back.at[i, 0], out.at[0, :, pl.ds(chunk_at(i), CHUNK)], own_sem.at[i]
        )

    def give_back(i):
        sl = pl.ds(EDGE + actual(16 + CHUNK * i), CHUNK)
        for name in ("u", "v", "s1", "s2", "s12"):
            edges = edge[name][0, sl]
            t[name][0, sl] = jnp.where(lane < DEEP, pltpu.roll(edges, BW - 16, 1), t[name][0, sl])
            t[name][NP - 1, sl] = jnp.where(
                lane >= BW - DEEP, pltpu.roll(edges, 32, 1), t[name][NP - 1, sl]
            )

        def fill(k):
            at = inverse[3, 0, k]
            back[i, k, 0] = t["u"][at, sl]
            back[i, k, 1] = t["v"][at, sl]
            back[i, k, 2] = t["s1"][at, sl]
            back[i, k, 3] = t["s2"][at, sl] * 0.25
            back[i, k, 4] = t["s12"][at, sl] * 0.125
            at = inverse[3, 1, k]
            diff_x = t["u"][at, sl] - t["uo"][at, sl]
            diff_y = t["v"][at, sl] - t["vo"][at, sl]
            square = diff_x * diff_x + diff_y * diff_y + 0.01
            drag = t["ac"][at, sl] * (square * lax.rsqrt(square))
            back[i, k, 5] = drag * diff_x
            back[i, k, 6] = drag * diff_y

        def one(k):
            fill(k)
            back_copy(i, k).start()

        each(1, one, unroll=5)
        fill(0)
        own_copy(i).start()

    def own(i):
        place(0, recv[i], actual(OWN_ROW[i]))
        send_sides(SIDE_OWN[i])

    def other(i):
        place_halo(i)
        send_sides(SIDE_HALO[i])

    for i in range(2):
        forward(i, 0)
        arrive(i, 1, NP)
        own(i)
        other(i)
    forward(2, 0)

    def beside_first(n):
        @pl.when(n >= 4)
        def _():
            arrive(2, jnp.maximum(4 * n - 16, 1), 4 * n - 12)

    first_waves(beside_first)
    own(2)
    forward(3, 0)
    for m in range(4):
        take_sides(m, SIDE_ROW[m])

    def beside_second(n):
        @pl.when(n > 0)
        def _():
            arrive(3, n, n + 1)

    wave(32, beside_second, 24, 4)
    other(2)
    take_sides(4, 32)
    strip_wave(32, lambda n: arrive(3, ITERS + n, ITERS + n + 1))
    own(3)
    give_back(0)

    def last_waves(i):
        @pl.when(i > 1)
        def _():
            take_sides(3 + i, 24 + 8 * i)

        wave(32 + 8 * i, lambda n: None, 24 + 8 * i, 1, jnp.where(i == 1, 1, 0))

        @pl.when(i == 1)
        def _():
            other(3)

        @pl.when(i > 1)
        def _():
            give_back(i - 1)

    each(1, last_waves, NC)
    take_sides(7, 56)
    strip_wave(56, lambda n: None)
    give_back(3)

    def drain(k):
        id_copy(k).wait_send()
        for i in range(NC):
            data_copy(i, k).wait_send()

    each(1, drain)

    @pl.when(has_up)
    def _():
        id_forward(0).wait_send()

        def one(k):
            for i in range(2):
                halo_copy(i, k).wait_send()

        each(0, one)

    id_forward(1).wait_send()

    def drain_low(k):
        for i in range(2, NC):
            halo_copy(i, k).wait_send()

    each(0, drain_low)
    for e in range(2):

        @pl.when((gy < NP - 1, gy > 0)[e])
        def _():
            for m in range(NS):
                side_copy(m, e).wait_send()

    for i in range(NC):
        own_copy(i).wait()
        each(1, lambda k: back_copy(i, k).wait_recv())
    for i in range(NC):
        each(1, lambda k: back_copy(i, k).wait_send())


def to_slots(omap, imap, held, ice_out, ocean_out, sem):
    gy = lax.axis_index("gy")
    x, z = lax.div(gy, 4), lax.rem(gy, 4)
    copies = []
    for n, (blocks, fields, out) in enumerate(
        ((imap, pl.ds(0, 5), ice_out), (omap, pl.ds(5, 2), ocean_out))
    ):
        for s in range(NP):
            c = tile_col(blocks[s])
            cx, cz = lax.div(c, 4), lax.rem(c, 4)
            k = lax.rem(cx - x + 4, 4) * 4 + lax.rem(cz - z + 4, 4)
            copies.append(pltpu.make_async_copy(held.at[k, fields], out.at[s], sem.at[n, s]))
            copies[-1].start()
    for copy in copies:
        copy.wait()


def shards(ocean_state, land_mask, ocean_map, ice_motion, ice_mass, ice_strength, ice_mask, ice_map):
    dma = pltpu.SemaphoreType.DMA
    vmem = pltpu.VMEM
    hbm = pl.BlockSpec(memory_space=pltpu.HBM)
    smem = pl.BlockSpec(memory_space=pltpu.SMEM)
    held = pl.BlockSpec(memory_space=pltpu.VMEM)
    integers = jnp.int32
    ids = vmem((NP, 8, BW), integers)

    def each_stage(shape, dtype):
        return [vmem(shape, dtype) for _ in range(NC)]

    held_back = pl.pallas_call(
        body,
        out_shape=jax.ShapeDtypeStruct((NP, RESULTS, BH, BW), F32),
        in_specs=[hbm] * 8,
        out_specs=hbm,
        scratch_shapes=[
            vmem((1, NP), integers),
            vmem((1, NP), integers),
            each_stage((NP, 4, CHUNK, BW), F32),
            each_stage((NP, CHUNK, BW), integers),
            each_stage((NP, 5, CHUNK, BW), F32),
            each_stage((NP, CHUNK, BW), F32),
            each_stage((NP, CHUNK, BW), F32),
            each_stage((NP, CHUNK, BW), integers),
            vmem((NC, NP, NF, CHUNK, BW), F32),
            each_stage((NP, NF, CHUNK, BW), F32),
            each_stage((NP, NF, CHUNK, BW), F32),
            ids, ids, ids, ids,
            vmem((8, BW), integers),
            vmem((4, 8, BW), integers),
            pltpu.SMEM((8, BW), integers),
            pltpu.SMEM((4, 8, BW), integers),
            vmem((NS, 2, 2, 8, BW), F32),
            vmem((NS, 2, 2, 8, BW), F32),
            vmem((NC, NP, RESULTS, CHUNK, BW), F32),
            [vmem((NP, ROWS, BW), F32) for _ in TILE_FIELDS],
            [vmem((2, ROWS, BW), F32) for _ in TILE_FIELDS],
            dma((NC, 6)), dma((2,)), dma((NP,)), dma((NP,)), dma((2,)), dma((2,)), dma((5,)),
            dma((NC, NP)), dma((NC, NP)), dma((NC, NP)), dma((NC, NP)),
            dma((NS, 2)), dma((NS, 2)), dma((NC, NP)), dma((NC, NP)), dma((NC,)),
        ],
        compiler_params=pltpu.CompilerParams(
            collective_id=0, has_side_effects=True, vmem_limit_bytes=48 << 20
        ),
        cost_estimate=pl.CostEstimate(flops=100_000_000, bytes_accessed=6 << 20, transcendentals=0),
        name="ice_subcycles",
    )(*[
        pltpu.with_memory_space_constraint(array, pltpu.HBM)
        for array in (
            ocean_map[None], ice_map[None], ocean_state, land_mask,
            ice_motion, ice_mass, ice_strength, ice_mask,
        )
    ])
    return pl.pallas_call(
        to_slots,
        out_shape=(
            jax.ShapeDtypeStruct((NP, 5, BH, BW), F32),
            jax.ShapeDtypeStruct((NP, 2, BH, BW), F32),
        ),
        in_specs=[smem, smem, held],
        out_specs=(hbm, hbm),
        scratch_shapes=[
            dma((2, NP)),
        ],
        compiler_params=pltpu.CompilerParams(vmem_limit_bytes=16 << 20),
        name="to_slots",
    )(ocean_map, ice_map, held_back)


def solution(mesh):
    blocks = P(("gx", "gy"), None, None, None)
    layer = P(("gx", "gy"), None, None)
    slots = P(("gx", "gy"))
    return jax.shard_map(
        shards, mesh=mesh,
        in_specs=(blocks, layer, slots, blocks, layer, layer, layer, slots),
        out_specs=(blocks, blocks), check_vma=False,
    )
```

```python
import functools

import jax
import jax.numpy as jnp
from jax import lax
from jax.experimental import pallas as pl
from jax.experimental.pallas import tpu as pltpu
from jax.sharding import PartitionSpec as P

BH = 32
BW = 128
NP = 16
NX = 8
ITERS = 8
DEEP = 16
HIGH = BH + 2 * DEEP
EDGE = 24
CHUNK = 8
NC = BH // CHUNK
ROWS = HIGH + 2 * EDGE
MESH = pl.DeviceIdType.MESH
F32 = jnp.float32

ICE = ("u", "v", "p", "s1", "s2", "s12", "m")
OCEAN = ("uo", "vo", "tx", "ty", "ac")
FIELDS = ICE + OCEAN
NF = len(FIELDS)
SIDE_SETS = (FIELDS[:6], FIELDS[6:])
TILE_FIELDS = FIELDS + ("sa", "sc")
RESULTS = 7
OWN_ROW = (16, 24, 32, 40)
HALO_ROW = (8, 0, 56, 48)
SIDE_ROW = (16, 8, 24, 0, 32, 40, 48, 56)
SIDE_OWN = (0, 2, 4, 5)
SIDE_HALO = (1, 3, 7, 6)
NS = len(SIDE_ROW)
FAR_FIRST = (10, 2, 8, 6, 14, 9, 11, 5, 15, 7, 13, 1, 4, 3, 12)


def shifted(col, k, sign):
    dx, dz = lax.div(k, 4), lax.rem(k, 4)
    x, z = lax.div(col, 4), lax.rem(col, 4)
    return lax.rem(x + sign * dx + 4, 4) * 4 + lax.rem(z + sign * dz + 4, 4)


def tile_col(block_id):
    return lax.rem(lax.div(block_id, NP), NP)


def x_difference(ref, off, j, lane):
    sl = pl.ds(EDGE + off, 8)
    here = ref[j, sl]
    if not isinstance(j, int):
        return pltpu.roll(here, BW - 1, 1) - pltpu.roll(here, 1, 1)
    up = pltpu.roll(jnp.where(lane == 0, ref[(j + 1) % NP, sl], here), BW - 1, 1)
    down = pltpu.roll(jnp.where(lane == BW - 1, ref[(j - 1) % NP, sl], here), 1, 1)
    return up - down


def y_difference(ref, off, j):
    return ref[j, pl.ds(EDGE + off + 1, 8)] - ref[j, pl.ds(EDGE + off - 1, 8)]


def stress_rows(t, off, j, lane):
    sl = pl.ds(EDGE + off, 8)
    east = x_difference(t["u"], off, j, lane)
    north = y_difference(t["v"], off, j)
    shear = y_difference(t["u"], off, j) + x_difference(t["v"], off, j, lane)
    diverg = east + north
    tension = east - north
    square = diverg * diverg + (tension * tension + shear * shear) * 0.25 + 0.16
    p = t["p"][j, sl]
    ratio = p * lax.rsqrt(square)
    s1 = 0.4 * t["s1"][j, sl] + (ratio * diverg - p)
    s2 = 0.4 * t["s2"][j, sl] + ratio * tension
    s12 = 0.4 * t["s12"][j, sl] + ratio * shear
    quarter = 0.25 * s2
    t["s1"][j, sl] = s1
    t["s2"][j, sl] = s2
    t["s12"][j, sl] = s12
    t["sa"][j, sl] = s1 + quarter
    t["sc"][j, sl] = s1 - quarter


def momentum_rows(t, off, j, lane):
    sl = pl.ds(EDGE + off, 8)
    force_x = x_difference(t["sa"], off, j, lane) * 0.25 + y_difference(t["s12"], off, j) * 0.0625
    force_y = x_difference(t["s12"], off, j, lane) * 0.0625 + y_difference(t["sc"], off, j) * 0.25
    u, v, m = t["u"][j, sl], t["v"][j, sl], t["m"][j, sl]
    uo, vo = t["uo"][j, sl], t["vo"][j, sl]
    diff_x, diff_y = uo - u, vo - v
    square = diff_x * diff_x + diff_y * diff_y + 0.01
    drag = square * lax.rsqrt(square)
    diag = m + drag
    rotate = 0.5 * m
    rhs_x = m * (u - t["tx"][j, sl]) + force_x + drag * uo
    rhs_y = m * (v - t["ty"][j, sl]) + force_y + drag * vo
    scale = t["ac"][j, sl] * pltpu.reciprocal(diag * diag + rotate * rotate, approx=True)
    t["u"][j, sl] = (diag * rhs_x + rotate * rhs_y) * scale
    t["v"][j, sl] = (diag * rhs_y - rotate * rhs_x) * scale


def body(
    omap_h, imap_h, ocean_h, land_h, motion_h, mass_h, strength_h, mask_h,
    out,
    omap, imap, ocean, land, motion, mass, strength, mask,
    send, recv, halo, ids_send, ids_recv, ids_up, ids_low, order_v, inverse_v,
    order, inverse, side_send, side_recv, back, tile, strip,
    in_sem, map_sem, id_s, id_r, idf_s, idf_r, small_sem, data_s, data_r,
    halo_s, halo_r, side_s, side_r, back_s, back_r, own_sem,
):
    gx, gy = lax.axis_index("gx"), lax.axis_index("gy")
    odd = lax.rem(gx, 2)
    sign = 1 - 2 * odd
    up, low = gx - sign, gx + sign
    has_up = (gx > 0) & (gx < NX - 1)
    t = dict(zip(TILE_FIELDS, tile))
    edge = dict(zip(TILE_FIELDS, strip))
    lane = lax.broadcasted_iota(jnp.int32, (8, BW), 1)
    row8 = lax.broadcasted_iota(jnp.int32, (8, BW), 0)

    def actual(row):
        return odd * (HIGH - 8) + sign * row

    def chunk_at(i):
        return odd * (BH - CHUNK) + sign * (CHUNK * i)

    barrier = pltpu.get_barrier_semaphore()

    def greet(k, _):
        pl.semaphore_signal(barrier, inc=1, device_id=(gx, shifted(gy, k, 1)), device_id_type=MESH)
        return 0

    lax.fori_loop(1, NP, greet, 0)
    for d in (1, NX - 1):
        pl.semaphore_signal(
            barrier, inc=1, device_id=(lax.rem(gx + d, NX), gy), device_id_type=MESH
        )
    map_loads = [
        pltpu.make_async_copy(imap_h, imap, map_sem.at[0]),
        pltpu.make_async_copy(omap_h, omap, map_sem.at[1]),
    ]
    loads = []
    for i in range(NC):
        rows = pl.ds(chunk_at(i), CHUNK)
        loads.append([
            pltpu.make_async_copy(motion_h.at[:, :, rows], motion[i], in_sem.at[i, 0]),
            pltpu.make_async_copy(strength_h.at[:, rows], strength[i], in_sem.at[i, 1]),
            pltpu.make_async_copy(mass_h.at[:, rows], mass[i], in_sem.at[i, 2]),
            pltpu.make_async_copy(mask_h.at[:, rows], mask[i], in_sem.at[i, 3]),
            pltpu.make_async_copy(ocean_h.at[:, :, rows], ocean[i], in_sem.at[i, 4]),
            pltpu.make_async_copy(land_h.at[:, rows], land[i], in_sem.at[i, 5]),
        ])
    for load in map_loads + sum(loads, []):
        load.start()
    for load in map_loads:
        load.wait()

    tile_of = lax.broadcasted_iota(jnp.int32, (NP, NP), 0)
    slot_of = lax.broadcasted_iota(jnp.int32, (NP, NP), 1)
    places = []
    found = jnp.zeros((8, BW), jnp.int32)
    lane16 = lax.broadcasted_iota(jnp.int32, (NP, BW), 1)
    row16 = lax.broadcasted_iota(jnp.int32, (NP, BW), 0)
    for row, blocks in ((0, imap), (1, omap)):
        block = jnp.broadcast_to(blocks[...], (NP, NP))
        same = tile_col(block) == tile_of
        slot = jnp.max(jnp.where(same, slot_of, 0), axis=1, keepdims=True)
        place_in = jnp.max(jnp.where(same, lax.rem(block, NP), 0), axis=1, keepdims=True)
        slot = jnp.broadcast_to(slot, (NP, BW))
        slot = jnp.max(jnp.where(lane16 == row16, slot, 0), axis=0, keepdims=True)
        found = jnp.where(row8 == row, slot, found)
        places.append(jnp.broadcast_to(place_in, (NP, BW)))
    order_v[...] = found
    order_copy = pltpu.make_async_copy(order_v, order, small_sem.at[0])
    order_copy.start()
    for c in range(NP):
        ids_send[c] = jnp.where(row8 == 0, places[0][c : c + 1], places[1][c : c + 1])
    ids_recv[0] = ids_send[gy]
    order_copy.wait()

    def packed(i, name, si, so):
        if name == "p":
            return strength[i][si] * 0.3
        if name == "m":
            return mass[i][si] * mask[i][si].astype(F32)
        if name == "ac":
            return (1 - land[i][so]).astype(F32)
        if name in ("u", "v", "s1"):
            return motion[i][si, ("u", "v", "s1").index(name)]
        if name == "s2":
            return motion[i][si, 3] * 4.0
        if name == "s12":
            return motion[i][si, 4] * 8.0
        return ocean[i][so, ("uo", "vo", "tx", "ty").index(name)]

    def each(lo, fn, hi=NP, unroll=None):
        def step(k, _):
            fn(k)
            return 0

        lax.fori_loop(lo, hi, step, 0, unroll=unroll)

    def mirrored(k):
        return k + odd * ((4 - k // 4) % 4 * 4 + (4 - k % 4) % 4 - k)

    def pack_and_send(i):
        def one(k):
            c = shifted(gy, k, 1)
            si, so = order[0, c], order[1, c]
            for f, name in enumerate(FIELDS):
                send[i, k, f] = packed(i, name, si, so)
            data_copy(i, k).start()

        for k in FAR_FIRST:
            one(mirrored(k))
        si, so = order[0, gy], order[1, gy]
        for f, name in enumerate(FIELDS):
            recv[i][0, f] = packed(i, name, si, so)

    def data_copy(i, k):
        return pltpu.make_async_remote_copy(
            src_ref=send.at[i, k], dst_ref=recv[i].at[k],
            send_sem=data_s.at[i, k], recv_sem=data_r.at[i, k],
            device_id=(gx, shifted(gy, k, 1)), device_id_type=MESH,
        )

    def id_copy(k):
        return pltpu.make_async_remote_copy(
            src_ref=ids_send.at[shifted(gy, k, 1)], dst_ref=ids_recv.at[k],
            send_sem=id_s.at[k], recv_sem=id_r.at[k],
            device_id=(gx, shifted(gy, k, 1)), device_id_type=MESH,
        )

    def halo_copy(i, k):
        return pltpu.make_async_remote_copy(
            src_ref=recv[i].at[k], dst_ref=halo[i].at[k],
            send_sem=halo_s.at[i, k], recv_sem=halo_r.at[i, k],
            device_id=(up if i < 2 else low, gy), device_id_type=MESH,
        )

    def id_forward(d):
        return pltpu.make_async_remote_copy(
            src_ref=ids_recv, dst_ref=(ids_up, ids_low)[d],
            send_sem=idf_s.at[d], recv_sem=idf_r.at[d],
            device_id=((up, low)[d], gy), device_id_type=MESH,
        )

    for i in range(NC):
        for load in loads[i]:
            load.wait()
        if i == 0:
            pl.semaphore_wait(barrier, NP - 1 + 2)
            each(1, lambda k: id_copy(k).start())
        pack_and_send(i)

    @pl.when(jnp.logical_not(has_up))
    def _():
        for name in FIELDS:
            t[name][:, pl.ds(EDGE + odd * (HIGH - DEEP), DEEP)] = jnp.zeros((NP, DEEP, BW), F32)

    for e in range(2):

        @pl.when(gy == (0, NP - 1)[e])
        def _():
            side_recv[:, e] = jnp.zeros((NS, 2, 8, BW), F32)

    each(1, lambda k: id_copy(k).wait_recv())

    @pl.when(has_up)
    def _():
        id_forward(0).start()

    id_forward(1).start()

    def invert(which, source):
        found = jnp.zeros((8, BW), jnp.int32)
        for k in range(NP):
            found = jnp.maximum(found, jnp.where(source[k] == lane, k, 0))
        inverse_v[which] = found
        copy = pltpu.make_async_copy(
            inverse_v.at[which], inverse.at[which], small_sem.at[1 + which]
        )
        copy.start()
        copy.wait()

    invert(0, ids_recv)
    place_of = jnp.zeros((8, BW), jnp.int32)
    for k in range(NP):
        place_of = jnp.where(lane == k, ids_recv[k], place_of)
    inverse_v[3] = place_of
    place_copy = pltpu.make_async_copy(inverse_v.at[3], inverse.at[3], small_sem.at[4])
    place_copy.start()
    place_copy.wait()

    @pl.when(has_up)
    def _():
        id_forward(0).wait_recv()
        invert(1, ids_up)

    id_forward(1).wait_recv()
    invert(2, ids_low)

    def forward(i, k):
        if i < 2:

            @pl.when(has_up)
            def _():
                halo_copy(i, k).start()

        else:
            halo_copy(i, k).start()

    def arrive(i, lo, hi):
        def one(k):
            data_copy(i, k).wait_recv()
            forward(i, k)

        each(lo, one, hi)

    def place(which, source, row):
        sl = pl.ds(EDGE + row, CHUNK)

        def one(j):
            si, so = inverse[which, 0, j], inverse[which, 1, j]
            for f, name in enumerate(FIELDS):
                value = source[si if name in ICE else so, f]
                if name == "ac":
                    value = jnp.where(source[si, FIELDS.index("m")] > 0.0, value, 0.0)
                t[name][j, sl] = value

        each(0, one, unroll=4)

    def place_halo(i):
        def take():
            each(0, lambda k: halo_copy(i, k).wait_recv())
            place(1 if i < 2 else 2, halo[i], actual(HALO_ROW[i]))

        if i < 2:
            pl.when(has_up)(take)
        else:
            take()

    def side_copy(m, e):
        return pltpu.make_async_remote_copy(
            src_ref=side_send.at[m, e], dst_ref=side_recv.at[m, e],
            send_sem=side_s.at[m, e], recv_sem=side_r.at[m, e],
            device_id=(gx, (gy + 1, gy - 1)[e]), device_id_type=MESH,
        )

    def send_sides(m):
        sl = pl.ds(EDGE + actual(SIDE_ROW[m]), CHUNK)
        for n, names in enumerate(SIDE_SETS):
            right = jnp.zeros((8, BW), F32)
            left = jnp.zeros((8, BW), F32)
            for f, name in enumerate(names):
                here = (lane >= DEEP * f) & (lane < DEEP * (f + 1))
                r = t[name][NP - 1, sl]
                q = t[name][0, sl]
                right = jnp.where(here, pltpu.roll(r, (DEEP * f + DEEP) % BW, 1), right)
                left = jnp.where(here, pltpu.roll(q, DEEP * f, 1) if f else q, left)
                first = jnp.where((lane >= 16) & (lane < 48), pltpu.roll(q, 16, 1), 0.0)
                last = pltpu.roll(r, BW - 32, 1)
                edge[name][0, sl] = jnp.where((lane >= 64) & (lane < 96), last, first)
            side_send[m, 0, n] = right
            side_send[m, 1, n] = left

        @pl.when(gy < NP - 1)
        def _():
            side_copy(m, 0).start()

        @pl.when(gy > 0)
        def _():
            side_copy(m, 1).start()

    def take_sides(m, row):
        @pl.when(gy > 0)
        def _():
            side_copy(m, 0).wait_recv()

        @pl.when(gy < NP - 1)
        def _():
            side_copy(m, 1).wait_recv()

        sl = pl.ds(EDGE + actual(row), CHUNK)
        for n, names in enumerate(SIDE_SETS):
            left = side_recv[m, 0, n]
            right = side_recv[m, 1, n]
            for f, name in enumerate(names):
                q = pltpu.roll(left, BW - DEEP * f, 1) if f else left
                r = pltpu.roll(right, 96 - DEEP * f, 1) if f < 6 else right
                value = jnp.where((lane >= 96) & (lane < 112), r, edge[name][0, sl])
                edge[name][0, sl] = jnp.where(lane < DEEP, q, value)

    def lowest(row, windows):
        return odd * (HIGH - 8) + sign * row - 8 * (windows - 1) * (1 - odd)

    def half_step(rows_of, row, windows=1, strip_row=None, strip_windows=1, strip_at=0):
        off = lowest(row, windows)
        for i in range(windows):
            for j in range(NP):
                rows_of(t, off + 8 * i, j, lane)
        if strip_row is not None:
            off = lowest(strip_row, strip_windows)
            for i in range(strip_windows):
                rows_of(edge, off + 8 * i, jnp.int32(strip_at), lane)

    def wave(end, beside, strip_end, strip_windows=1, strip_at=0):
        def one(n):
            h = 2 * n + 1
            half_step(stress_rows, end - h, 1, strip_end - h, strip_windows, strip_at)
            half_step(momentum_rows, end - h - 1, 1, strip_end - h - 1, strip_windows, strip_at)
            beside(n)

        each(0, one, ITERS)

    def first_waves(beside):
        def one(n):
            each(0, lambda i: half_step(stress_rows, 23 - 2 * n - 16 * i, 2), lax.div(45 - 4 * n, 16))
            each(0, lambda i: half_step(momentum_rows, 22 - 2 * n - 16 * i, 2), lax.div(43 - 4 * n, 16))
            beside(n)

        each(0, one, ITERS)

    def strip_wave(end, beside):
        def one(n):
            stress_rows(edge, actual(end - 2 * n - 1), jnp.int32(0), lane)
            momentum_rows(edge, actual(end - 2 * n - 2), jnp.int32(0), lane)
            beside(n)

        each(0, one, ITERS)

    def back_copy(i, k):
        return pltpu.make_async_remote_copy(
            src_ref=back.at[i, k], dst_ref=out.at[k, :, pl.ds(chunk_at(i), CHUNK)],
            send_sem=back_s.at[i, k], recv_sem=back_r.at[i, k],
            device_id=(gx, shifted(gy, k, -1)), device_id_type=MESH,
        )

    def own_copy(i):
        return pltpu.make_async_copy(
            back.at[i, 0], out.at[0, :, pl.ds(chunk_at(i), CHUNK)], own_sem.at[i]
        )

    def give_back(i):
        sl = pl.ds(EDGE + actual(16 + CHUNK * i), CHUNK)
        for name in ("u", "v", "s1", "s2", "s12"):
            edges = edge[name][0, sl]
            t[name][0, sl] = jnp.where(lane < DEEP, pltpu.roll(edges, BW - 16, 1), t[name][0, sl])
            t[name][NP - 1, sl] = jnp.where(
                lane >= BW - DEEP, pltpu.roll(edges, 32, 1), t[name][NP - 1, sl]
            )

        def fill(k):
            at = inverse[3, 0, k]
            back[i, k, 0] = t["u"][at, sl]
            back[i, k, 1] = t["v"][at, sl]
            back[i, k, 2] = t["s1"][at, sl]
            back[i, k, 3] = t["s2"][at, sl] * 0.25
            back[i, k, 4] = t["s12"][at, sl] * 0.125
            at = inverse[3, 1, k]
            diff_x = t["u"][at, sl] - t["uo"][at, sl]
            diff_y = t["v"][at, sl] - t["vo"][at, sl]
            square = diff_x * diff_x + diff_y * diff_y + 0.01
            drag = t["ac"][at, sl] * (square * lax.rsqrt(square))
            back[i, k, 5] = drag * diff_x
            back[i, k, 6] = drag * diff_y

        def one(k):
            fill(k)
            back_copy(i, k).start()

        for k in FAR_FIRST:
            one(mirrored(k))
        fill(0)
        own_copy(i).start()

    def own(i):
        place(0, recv[i], actual(OWN_ROW[i]))
        send_sides(SIDE_OWN[i])

    def other(i):
        place_halo(i)
        send_sides(SIDE_HALO[i])

    for i in range(2):
        forward(i, 0)
        arrive(i, 1, NP)
        own(i)
        other(i)
    forward(2, 0)

    def beside_first(n):
        @pl.when(n >= 4)
        def _():
            arrive(2, jnp.maximum(4 * n - 16, 1), 4 * n - 12)

    first_waves(beside_first)
    own(2)
    forward(3, 0)
    for m in range(4):
        take_sides(m, SIDE_ROW[m])

    def beside_second(n):
        @pl.when(n > 0)
        def _():
            arrive(3, n, n + 1)

    wave(32, beside_second, 24, 4)
    other(2)
    take_sides(4, 32)
    strip_wave(32, lambda n: arrive(3, ITERS + n, ITERS + n + 1))
    own(3)
    give_back(0)

    def last_waves(i):
        @pl.when(i > 1)
        def _():
            take_sides(3 + i, 24 + 8 * i)

        wave(32 + 8 * i, lambda n: None, 24 + 8 * i, 1, jnp.where(i == 1, 1, 0))

        @pl.when(i == 1)
        def _():
            other(3)

        @pl.when(i > 1)
        def _():
            give_back(i - 1)

    each(1, last_waves, NC)
    take_sides(7, 56)
    strip_wave(56, lambda n: None)
    give_back(3)

    def drain(k):
        id_copy(k).wait_send()
        for i in range(NC):
            data_copy(i, k).wait_send()

    each(1, drain)

    @pl.when(has_up)
    def _():
        id_forward(0).wait_send()

        def one(k):
            for i in range(2):
                halo_copy(i, k).wait_send()

        each(0, one)

    id_forward(1).wait_send()

    def drain_low(k):
        for i in range(2, NC):
            halo_copy(i, k).wait_send()

    each(0, drain_low)
    for e in range(2):

        @pl.when((gy < NP - 1, gy > 0)[e])
        def _():
            for m in range(NS):
                side_copy(m, e).wait_send()

    for i in range(NC):
        own_copy(i).wait()
        each(1, lambda k: back_copy(i, k).wait_send(), unroll=5)
        each(1, lambda k: back_copy(i, k).wait_recv(), unroll=5)


def to_slots(omap, imap, held, ice_out, ocean_out, sem):
    gy = lax.axis_index("gy")
    x, z = lax.div(gy, 4), lax.rem(gy, 4)
    copies = []
    for n, (blocks, fields, out) in enumerate(
        ((imap, pl.ds(0, 5), ice_out), (omap, pl.ds(5, 2), ocean_out))
    ):
        for s in range(NP):
            c = tile_col(blocks[s])
            cx, cz = lax.div(c, 4), lax.rem(c, 4)
            k = lax.rem(cx - x + 4, 4) * 4 + lax.rem(cz - z + 4, 4)
            copies.append(pltpu.make_async_copy(held.at[k, fields], out.at[s], sem.at[n, s]))
            copies[-1].start()
    for copy in copies:
        copy.wait()


def shards(ocean_state, land_mask, ocean_map, ice_motion, ice_mass, ice_strength, ice_mask, ice_map):
    dma = pltpu.SemaphoreType.DMA
    vmem = pltpu.VMEM
    hbm = pl.BlockSpec(memory_space=pltpu.HBM)
    smem = pl.BlockSpec(memory_space=pltpu.SMEM)
    held = pl.BlockSpec(memory_space=pltpu.VMEM)
    integers = jnp.int32
    ids = vmem((NP, 8, BW), integers)

    def each_stage(shape, dtype):
        return [vmem(shape, dtype) for _ in range(NC)]

    held_back = pl.pallas_call(
        body,
        out_shape=jax.ShapeDtypeStruct((NP, RESULTS, BH, BW), F32),
        in_specs=[hbm] * 8,
        out_specs=hbm,
        scratch_shapes=[
            vmem((1, NP), integers),
            vmem((1, NP), integers),
            each_stage((NP, 4, CHUNK, BW), F32),
            each_stage((NP, CHUNK, BW), integers),
            each_stage((NP, 5, CHUNK, BW), F32),
            each_stage((NP, CHUNK, BW), F32),
            each_stage((NP, CHUNK, BW), F32),
            each_stage((NP, CHUNK, BW), integers),
            vmem((NC, NP, NF, CHUNK, BW), F32),
            each_stage((NP, NF, CHUNK, BW), F32),
            each_stage((NP, NF, CHUNK, BW), F32),
            ids, ids, ids, ids,
            vmem((8, BW), integers),
            vmem((4, 8, BW), integers),
            pltpu.SMEM((8, BW), integers),
            pltpu.SMEM((4, 8, BW), integers),
            vmem((NS, 2, 2, 8, BW), F32),
            vmem((NS, 2, 2, 8, BW), F32),
            vmem((NC, NP, RESULTS, CHUNK, BW), F32),
            [vmem((NP, ROWS, BW), F32) for _ in TILE_FIELDS],
            [vmem((2, ROWS, BW), F32) for _ in TILE_FIELDS],
            dma((NC, 6)), dma((2,)), dma((NP,)), dma((NP,)), dma((2,)), dma((2,)), dma((5,)),
            dma((NC, NP)), dma((NC, NP)), dma((NC, NP)), dma((NC, NP)),
            dma((NS, 2)), dma((NS, 2)), dma((NC, NP)), dma((NC, NP)), dma((NC,)),
        ],
        compiler_params=pltpu.CompilerParams(
            collective_id=0, has_side_effects=True, vmem_limit_bytes=48 << 20
        ),
        cost_estimate=pl.CostEstimate(flops=100_000_000, bytes_accessed=6 << 20, transcendentals=0),
        name="ice_subcycles",
    )(*[
        pltpu.with_memory_space_constraint(array, pltpu.HBM)
        for array in (
            ocean_map[None], ice_map[None], ocean_state, land_mask,
            ice_motion, ice_mass, ice_strength, ice_mask,
        )
    ])
    return pl.pallas_call(
        to_slots,
        out_shape=(
            jax.ShapeDtypeStruct((NP, 5, BH, BW), F32),
            jax.ShapeDtypeStruct((NP, 2, BH, BW), F32),
        ),
        in_specs=[smem, smem, held],
        out_specs=(hbm, hbm),
        scratch_shapes=[
            dma((2, NP)),
        ],
        compiler_params=pltpu.CompilerParams(vmem_limit_bytes=16 << 20),
        name="to_slots",
    )(ocean_map, ice_map, held_back)


def solution(mesh):
    blocks = P(("gx", "gy"), None, None, None)
    layer = P(("gx", "gy"), None, None)
    slots = P(("gx", "gy"))
    return jax.shard_map(
        shards, mesh=mesh,
        in_specs=(blocks, layer, slots, blocks, layer, layer, layer, slots),
        out_specs=(blocks, blocks), check_vma=False,
    )
```

```python
import functools

import jax
import jax.numpy as jnp
from jax import lax
from jax.experimental import pallas as pl
from jax.experimental.pallas import tpu as pltpu
from jax.sharding import PartitionSpec as P

BH = 32
BW = 128
NP = 16
NX = 8
ITERS = 8
DEEP = 16
HIGH = BH + 2 * DEEP
EDGE = 24
CHUNK = 8
NC = BH // CHUNK
ROWS = HIGH + 2 * EDGE
MESH = pl.DeviceIdType.MESH
F32 = jnp.float32

ICE = ("u", "v", "p", "s1", "s2", "s12", "m")
OCEAN = ("uo", "vo", "tx", "ty", "ac")
FIELDS = ICE + OCEAN
NF = len(FIELDS)
SIDE_SETS = (FIELDS[:6], FIELDS[6:])
TILE_FIELDS = FIELDS + ("sa", "sc")
RESULTS = 7
OWN_ROW = (16, 24, 32, 40)
HALO_ROW = (8, 0, 56, 48)
SIDE_ROW = (16, 8, 24, 0, 32, 40, 48, 56)
SIDE_OWN = (0, 2, 4, 5)
SIDE_HALO = (1, 3, 7, 6)
NS = len(SIDE_ROW)
FAR_FIRST = (10, 2, 8, 6, 14, 9, 11, 5, 15, 7, 13, 1, 4, 3, 12)


def shifted(col, k, sign):
    dx, dz = lax.div(k, 4), lax.rem(k, 4)
    x, z = lax.div(col, 4), lax.rem(col, 4)
    return lax.rem(x + sign * dx + 4, 4) * 4 + lax.rem(z + sign * dz + 4, 4)


def tile_col(block_id):
    return lax.rem(lax.div(block_id, NP), NP)


def x_difference(ref, off, j, lane):
    sl = pl.ds(EDGE + off, 8)
    here = ref[j, sl]
    if not isinstance(j, int):
        return pltpu.roll(here, BW - 1, 1) - pltpu.roll(here, 1, 1)
    up = pltpu.roll(jnp.where(lane == 0, ref[(j + 1) % NP, sl], here), BW - 1, 1)
    down = pltpu.roll(jnp.where(lane == BW - 1, ref[(j - 1) % NP, sl], here), 1, 1)
    return up - down


def y_difference(ref, off, j):
    return ref[j, pl.ds(EDGE + off + 1, 8)] - ref[j, pl.ds(EDGE + off - 1, 8)]


def stress_rows(t, off, j, lane):
    sl = pl.ds(EDGE + off, 8)
    east = x_difference(t["u"], off, j, lane)
    north = y_difference(t["v"], off, j)
    shear = y_difference(t["u"], off, j) + x_difference(t["v"], off, j, lane)
    diverg = east + north
    tension = east - north
    square = diverg * diverg + (tension * tension + shear * shear) * 0.25 + 0.16
    p = t["p"][j, sl]
    ratio = p * lax.rsqrt(square)
    s1 = 0.4 * t["s1"][j, sl] + (ratio * diverg - p)
    s2 = 0.4 * t["s2"][j, sl] + ratio * tension
    s12 = 0.4 * t["s12"][j, sl] + ratio * shear
    quarter = 0.25 * s2
    t["s1"][j, sl] = s1
    t["s2"][j, sl] = s2
    t["s12"][j, sl] = s12
    t["sa"][j, sl] = s1 + quarter
    t["sc"][j, sl] = s1 - quarter


def momentum_rows(t, off, j, lane):
    sl = pl.ds(EDGE + off, 8)
    force_x = x_difference(t["sa"], off, j, lane) * 0.25 + y_difference(t["s12"], off, j) * 0.0625
    force_y = x_difference(t["s12"], off, j, lane) * 0.0625 + y_difference(t["sc"], off, j) * 0.25
    u, v, m = t["u"][j, sl], t["v"][j, sl], t["m"][j, sl]
    uo, vo = t["uo"][j, sl], t["vo"][j, sl]
    diff_x, diff_y = uo - u, vo - v
    square = diff_x * diff_x + diff_y * diff_y + 0.01
    drag = square * lax.rsqrt(square)
    diag = m + drag
    rotate = 0.5 * m
    rhs_x = m * (u - t["tx"][j, sl]) + force_x + drag * uo
    rhs_y = m * (v - t["ty"][j, sl]) + force_y + drag * vo
    scale = t["ac"][j, sl] * pltpu.reciprocal(diag * diag + rotate * rotate, approx=True)
    t["u"][j, sl] = (diag * rhs_x + rotate * rhs_y) * scale
    t["v"][j, sl] = (diag * rhs_y - rotate * rhs_x) * scale


def body(
    omap_h, imap_h, ocean_h, land_h, motion_h, mass_h, strength_h, mask_h,
    out,
    omap, imap, ocean, land, motion, mass, strength, mask,
    send, recv, halo, ids_send, ids_recv, ids_up, ids_low, order_v, inverse_v,
    order, inverse, side_send, side_recv, back, tile, strip,
    in_sem, map_sem, id_s, id_r, idf_s, idf_r, small_sem, data_s, data_r,
    halo_s, halo_r, side_s, side_r, back_s, back_r, own_sem,
):
    gx, gy = lax.axis_index("gx"), lax.axis_index("gy")
    odd = lax.rem(gx, 2)
    sign = 1 - 2 * odd
    up, low = gx - sign, gx + sign
    has_up = (gx > 0) & (gx < NX - 1)
    t = dict(zip(TILE_FIELDS, tile))
    edge = dict(zip(TILE_FIELDS, strip))
    lane = lax.broadcasted_iota(jnp.int32, (8, BW), 1)
    row8 = lax.broadcasted_iota(jnp.int32, (8, BW), 0)

    def actual(row):
        return odd * (HIGH - 8) + sign * row

    def chunk_at(i):
        return odd * (BH - CHUNK) + sign * (CHUNK * i)

    map_loads = [
        pltpu.make_async_copy(imap_h, imap, map_sem.at[0]),
        pltpu.make_async_copy(omap_h, omap, map_sem.at[1]),
    ]
    for load in map_loads:
        load.start()

    barrier = pltpu.get_barrier_semaphore()

    def greet(k, _):
        pl.semaphore_signal(barrier, inc=1, device_id=(gx, shifted(gy, k, 1)), device_id_type=MESH)
        return 0

    lax.fori_loop(1, NP, greet, 0)
    for d in (1, NX - 1):
        pl.semaphore_signal(
            barrier, inc=1, device_id=(lax.rem(gx + d, NX), gy), device_id_type=MESH
        )
    loads = []
    for i in range(NC):
        rows = pl.ds(chunk_at(i), CHUNK)
        loads.append([
            pltpu.make_async_copy(motion_h.at[:, :, rows], motion[i], in_sem.at[i, 0]),
            pltpu.make_async_copy(strength_h.at[:, rows], strength[i], in_sem.at[i, 1]),
            pltpu.make_async_copy(mass_h.at[:, rows], mass[i], in_sem.at[i, 2]),
            pltpu.make_async_copy(mask_h.at[:, rows], mask[i], in_sem.at[i, 3]),
            pltpu.make_async_copy(ocean_h.at[:, :, rows], ocean[i], in_sem.at[i, 4]),
            pltpu.make_async_copy(land_h.at[:, rows], land[i], in_sem.at[i, 5]),
        ])
    for load in loads[0]:
        load.start()
    for load in map_loads:
        load.wait()

    tile_of = lax.broadcasted_iota(jnp.int32, (NP, NP), 0)
    slot_of = lax.broadcasted_iota(jnp.int32, (NP, NP), 1)
    places = []
    found = jnp.zeros((8, BW), jnp.int32)
    lane16 = lax.broadcasted_iota(jnp.int32, (NP, BW), 1)
    row16 = lax.broadcasted_iota(jnp.int32, (NP, BW), 0)
    for row, blocks in ((0, imap), (1, omap)):
        block = jnp.broadcast_to(blocks[...], (NP, NP))
        same = tile_col(block) == tile_of
        slot = jnp.max(jnp.where(same, slot_of, 0), axis=1, keepdims=True)
        place_in = jnp.max(jnp.where(same, lax.rem(block, NP), 0), axis=1, keepdims=True)
        slot = jnp.broadcast_to(slot, (NP, BW))
        slot = jnp.max(jnp.where(lane16 == row16, slot, 0), axis=0, keepdims=True)
        found = jnp.where(row8 == row, slot, found)
        places.append(jnp.broadcast_to(place_in, (NP, BW)))
    order_v[...] = found
    order_copy = pltpu.make_async_copy(order_v, order, small_sem.at[0])
    order_copy.start()
    for c in range(NP):
        ids_send[c] = jnp.where(row8 == 0, places[0][c : c + 1], places[1][c : c + 1])
    ids_recv[0] = ids_send[gy]
    order_copy.wait()

    def packed(i, name, si, so):
        if name == "p":
            return strength[i][si] * 0.3
        if name == "m":
            return mass[i][si] * mask[i][si].astype(F32)
        if name == "ac":
            return (1 - land[i][so]).astype(F32)
        if name in ("u", "v", "s1"):
            return motion[i][si, ("u", "v", "s1").index(name)]
        if name == "s2":
            return motion[i][si, 3] * 4.0
        if name == "s12":
            return motion[i][si, 4] * 8.0
        return ocean[i][so, ("uo", "vo", "tx", "ty").index(name)]

    def each(lo, fn, hi=NP, unroll=None):
        def step(k, _):
            fn(k)
            return 0

        lax.fori_loop(lo, hi, step, 0, unroll=unroll)

    def mirrored(k):
        return k + odd * ((4 - k // 4) % 4 * 4 + (4 - k % 4) % 4 - k)

    def pack_and_send(i):
        def one(k):
            c = shifted(gy, k, 1)
            si, so = order[0, c], order[1, c]
            for f, name in enumerate(FIELDS):
                send[i, k, f] = packed(i, name, si, so)
            data_copy(i, k).start()

        for k in FAR_FIRST:
            one(mirrored(k))
        si, so = order[0, gy], order[1, gy]
        for f, name in enumerate(FIELDS):
            recv[i][0, f] = packed(i, name, si, so)

    def data_copy(i, k):
        return pltpu.make_async_remote_copy(
            src_ref=send.at[i, k], dst_ref=recv[i].at[k],
            send_sem=data_s.at[i, k], recv_sem=data_r.at[i, k],
            device_id=(gx, shifted(gy, k, 1)), device_id_type=MESH,
        )

    def id_copy(k):
        return pltpu.make_async_remote_copy(
            src_ref=ids_send.at[shifted(gy, k, 1)], dst_ref=ids_recv.at[k],
            send_sem=id_s.at[k], recv_sem=id_r.at[k],
            device_id=(gx, shifted(gy, k, 1)), device_id_type=MESH,
        )

    def halo_copy(i, k):
        return pltpu.make_async_remote_copy(
            src_ref=recv[i].at[k], dst_ref=halo[i].at[k],
            send_sem=halo_s.at[i, k], recv_sem=halo_r.at[i, k],
            device_id=(up if i < 2 else low, gy), device_id_type=MESH,
        )

    def id_forward(d):
        return pltpu.make_async_remote_copy(
            src_ref=ids_recv, dst_ref=(ids_up, ids_low)[d],
            send_sem=idf_s.at[d], recv_sem=idf_r.at[d],
            device_id=((up, low)[d], gy), device_id_type=MESH,
        )

    for i in range(NC):
        for load in loads[i]:
            load.wait()
        if i == 0:
            pl.semaphore_wait(barrier, NP - 1 + 2)
            each(1, lambda k: id_copy(k).start())
        pack_and_send(i)
        if i == 0:
            for load in sum(loads[1:], []):
                load.start()

    @pl.when(jnp.logical_not(has_up))
    def _():
        for name in FIELDS:
            t[name][:, pl.ds(EDGE + odd * (HIGH - DEEP), DEEP)] = jnp.zeros((NP, DEEP, BW), F32)

    for e in range(2):

        @pl.when(gy == (0, NP - 1)[e])
        def _():
            side_recv[:, e] = jnp.zeros((NS, 2, 8, BW), F32)

    each(1, lambda k: id_copy(k).wait_recv())

    @pl.when(has_up)
    def _():
        id_forward(0).start()

    id_forward(1).start()

    def invert(which, source):
        found = jnp.zeros((8, BW), jnp.int32)
        for k in range(NP):
            found = jnp.maximum(found, jnp.where(source[k] == lane, k, 0))
        inverse_v[which] = found
        copy = pltpu.make_async_copy(
            inverse_v.at[which], inverse.at[which], small_sem.at[1 + which]
        )
        copy.start()
        copy.wait()

    invert(0, ids_recv)
    place_of = jnp.zeros((8, BW), jnp.int32)
    for k in range(NP):
        place_of = jnp.where(lane == k, ids_recv[k], place_of)
    inverse_v[3] = place_of
    place_copy = pltpu.make_async_copy(inverse_v.at[3], inverse.at[3], small_sem.at[4])
    place_copy.start()
    place_copy.wait()

    @pl.when(has_up)
    def _():
        id_forward(0).wait_recv()
        invert(1, ids_up)

    id_forward(1).wait_recv()
    invert(2, ids_low)

    def forward(i, k):
        if i < 2:

            @pl.when(has_up)
            def _():
                halo_copy(i, k).start()

        else:
            halo_copy(i, k).start()

    def arrive(i, lo, hi):
        def one(k):
            data_copy(i, k).wait_recv()
            forward(i, k)

        each(lo, one, hi)

    def place(which, source, row):
        sl = pl.ds(EDGE + row, CHUNK)

        def one(j):
            si, so = inverse[which, 0, j], inverse[which, 1, j]
            for f, name in enumerate(FIELDS):
                value = source[si if name in ICE else so, f]
                if name == "ac":
                    value = jnp.where(source[si, FIELDS.index("m")] > 0.0, value, 0.0)
                t[name][j, sl] = value

        each(0, one, unroll=4)

    def place_halo(i):
        def take():
            each(0, lambda k: halo_copy(i, k).wait_recv())
            place(1 if i < 2 else 2, halo[i], actual(HALO_ROW[i]))

        if i < 2:
            pl.when(has_up)(take)
        else:
            take()

    def side_copy(m, e):
        return pltpu.make_async_remote_copy(
            src_ref=side_send.at[m, e], dst_ref=side_recv.at[m, e],
            send_sem=side_s.at[m, e], recv_sem=side_r.at[m, e],
            device_id=(gx, (gy + 1, gy - 1)[e]), device_id_type=MESH,
        )

    def send_sides(m):
        sl = pl.ds(EDGE + actual(SIDE_ROW[m]), CHUNK)
        for n, names in enumerate(SIDE_SETS):
            right = jnp.zeros((8, BW), F32)
            left = jnp.zeros((8, BW), F32)
            for f, name in enumerate(names):
                here = (lane >= DEEP * f) & (lane < DEEP * (f + 1))
                r = t[name][NP - 1, sl]
                q = t[name][0, sl]
                right = jnp.where(here, pltpu.roll(r, (DEEP * f + DEEP) % BW, 1), right)
                left = jnp.where(here, pltpu.roll(q, DEEP * f, 1) if f else q, left)
                first = jnp.where((lane >= 16) & (lane < 48), pltpu.roll(q, 16, 1), 0.0)
                last = pltpu.roll(r, BW - 32, 1)
                edge[name][0, sl] = jnp.where((lane >= 64) & (lane < 96), last, first)
            side_send[m, 0, n] = right
            side_send[m, 1, n] = left

        @pl.when(gy < NP - 1)
        def _():
            side_copy(m, 0).start()

        @pl.when(gy > 0)
        def _():
            side_copy(m, 1).start()

    def take_sides(m, row):
        @pl.when(gy > 0)
        def _():
            side_copy(m, 0).wait_recv()

        @pl.when(gy < NP - 1)
        def _():
            side_copy(m, 1).wait_recv()

        sl = pl.ds(EDGE + actual(row), CHUNK)
        for n, names in enumerate(SIDE_SETS):
            left = side_recv[m, 0, n]
            right = side_recv[m, 1, n]
            for f, name in enumerate(names):
                q = pltpu.roll(left, BW - DEEP * f, 1) if f else left
                r = pltpu.roll(right, 96 - DEEP * f, 1) if f < 6 else right
                value = jnp.where((lane >= 96) & (lane < 112), r, edge[name][0, sl])
                edge[name][0, sl] = jnp.where(lane < DEEP, q, value)

    def lowest(row, windows):
        return odd * (HIGH - 8) + sign * row - 8 * (windows - 1) * (1 - odd)

    def half_step(rows_of, row, windows=1, strip_row=None, strip_windows=1, strip_at=0):
        off = lowest(row, windows)
        for i in range(windows):
            for j in range(NP):
                rows_of(t, off + 8 * i, j, lane)
        if strip_row is not None:
            off = lowest(strip_row, strip_windows)
            for i in range(strip_windows):
                rows_of(edge, off + 8 * i, jnp.int32(strip_at), lane)

    def wave(end, beside, strip_end, strip_windows=1, strip_at=0):
        def one(n):
            h = 2 * n + 1
            half_step(stress_rows, end - h, 1, strip_end - h, strip_windows, strip_at)
            half_step(momentum_rows, end - h - 1, 1, strip_end - h - 1, strip_windows, strip_at)
            beside(n)

        each(0, one, ITERS)

    def first_waves(beside):
        def one(n):
            each(0, lambda i: half_step(stress_rows, 23 - 2 * n - 16 * i, 2), lax.div(45 - 4 * n, 16))
            each(0, lambda i: half_step(momentum_rows, 22 - 2 * n - 16 * i, 2), lax.div(43 - 4 * n, 16))
            beside(n)

        each(0, one, ITERS)

    def strip_wave(end, beside):
        def one(n):
            stress_rows(edge, actual(end - 2 * n - 1), jnp.int32(0), lane)
            momentum_rows(edge, actual(end - 2 * n - 2), jnp.int32(0), lane)
            beside(n)

        each(0, one, ITERS)

    def back_copy(i, k):
        return pltpu.make_async_remote_copy(
            src_ref=back.at[i, k], dst_ref=out.at[k, :, pl.ds(chunk_at(i), CHUNK)],
            send_sem=back_s.at[i, k], recv_sem=back_r.at[i, k],
            device_id=(gx, shifted(gy, k, -1)), device_id_type=MESH,
        )

    def own_copy(i):
        return pltpu.make_async_copy(
            back.at[i, 0], out.at[0, :, pl.ds(chunk_at(i), CHUNK)], own_sem.at[i]
        )

    def give_back(i):
        sl = pl.ds(EDGE + actual(16 + CHUNK * i), CHUNK)
        for name in ("u", "v", "s1", "s2", "s12"):
            edges = edge[name][0, sl]
            t[name][0, sl] = jnp.where(lane < DEEP, pltpu.roll(edges, BW - 16, 1), t[name][0, sl])
            t[name][NP - 1, sl] = jnp.where(
                lane >= BW - DEEP, pltpu.roll(edges, 32, 1), t[name][NP - 1, sl]
            )

        def fill(k):
            at = inverse[3, 0, k]
            back[i, k, 0] = t["u"][at, sl]
            back[i, k, 1] = t["v"][at, sl]
            back[i, k, 2] = t["s1"][at, sl]
            back[i, k, 3] = t["s2"][at, sl] * 0.25
            back[i, k, 4] = t["s12"][at, sl] * 0.125
            at = inverse[3, 1, k]
            diff_x = t["u"][at, sl] - t["uo"][at, sl]
            diff_y = t["v"][at, sl] - t["vo"][at, sl]
            square = diff_x * diff_x + diff_y * diff_y + 0.01
            drag = t["ac"][at, sl] * (square * lax.rsqrt(square))
            back[i, k, 5] = drag * diff_x
            back[i, k, 6] = drag * diff_y

        def one(k):
            fill(k)
            back_copy(i, k).start()

        for k in FAR_FIRST:
            one(mirrored(k))
        fill(0)
        own_copy(i).start()

    def own(i):
        place(0, recv[i], actual(OWN_ROW[i]))
        send_sides(SIDE_OWN[i])

    def other(i):
        place_halo(i)
        send_sides(SIDE_HALO[i])

    for i in range(2):
        forward(i, 0)
        arrive(i, 1, NP)
        own(i)
        other(i)
    forward(2, 0)

    def beside_first(n):
        @pl.when(n >= 4)
        def _():
            arrive(2, jnp.maximum(4 * n - 16, 1), 4 * n - 12)

    first_waves(beside_first)
    own(2)
    forward(3, 0)
    for m in range(4):
        take_sides(m, SIDE_ROW[m])

    def beside_second(n):
        @pl.when(n > 0)
        def _():
            arrive(3, n, n + 1)

    wave(32, beside_second, 24, 4)
    other(2)
    take_sides(4, 32)
    strip_wave(32, lambda n: arrive(3, ITERS + n, ITERS + n + 1))
    own(3)
    give_back(0)

    def last_waves(i):
        @pl.when(i > 1)
        def _():
            take_sides(3 + i, 24 + 8 * i)

        wave(32 + 8 * i, lambda n: None, 24 + 8 * i, 1, jnp.where(i == 1, 1, 0))

        @pl.when(i == 1)
        def _():
            other(3)

        @pl.when(i > 1)
        def _():
            give_back(i - 1)

    each(1, last_waves, NC)
    take_sides(7, 56)
    strip_wave(56, lambda n: None)
    give_back(3)

    def drain(k):
        id_copy(k).wait_send()
        for i in range(NC):
            data_copy(i, k).wait_send()

    each(1, drain)

    @pl.when(has_up)
    def _():
        id_forward(0).wait_send()

        def one(k):
            for i in range(2):
                halo_copy(i, k).wait_send()

        each(0, one)

    id_forward(1).wait_send()

    def drain_low(k):
        for i in range(2, NC):
            halo_copy(i, k).wait_send()

    each(0, drain_low)
    for e in range(2):

        @pl.when((gy < NP - 1, gy > 0)[e])
        def _():
            for m in range(NS):
                side_copy(m, e).wait_send()

    for i in range(NC):
        own_copy(i).wait()
        each(1, lambda k: back_copy(i, k).wait_send(), unroll=5)
        each(1, lambda k: back_copy(i, k).wait_recv(), unroll=5)


def to_slots(omap, imap, held, ice_out, ocean_out, sem):
    gy = lax.axis_index("gy")
    x, z = lax.div(gy, 4), lax.rem(gy, 4)
    copies = []
    for n, (blocks, fields, out) in enumerate(
        ((imap, pl.ds(0, 5), ice_out), (omap, pl.ds(5, 2), ocean_out))
    ):
        for s in range(NP):
            c = tile_col(blocks[s])
            cx, cz = lax.div(c, 4), lax.rem(c, 4)
            k = lax.rem(cx - x + 4, 4) * 4 + lax.rem(cz - z + 4, 4)
            copies.append(pltpu.make_async_copy(held.at[k, fields], out.at[s], sem.at[n, s]))
            copies[-1].start()
    for copy in copies:
        copy.wait()


def shards(ocean_state, land_mask, ocean_map, ice_motion, ice_mass, ice_strength, ice_mask, ice_map):
    dma = pltpu.SemaphoreType.DMA
    vmem = pltpu.VMEM
    hbm = pl.BlockSpec(memory_space=pltpu.HBM)
    smem = pl.BlockSpec(memory_space=pltpu.SMEM)
    held = pl.BlockSpec(memory_space=pltpu.VMEM)
    integers = jnp.int32
    ids = vmem((NP, 8, BW), integers)

    def each_stage(shape, dtype):
        return [vmem(shape, dtype) for _ in range(NC)]

    held_back = pl.pallas_call(
        body,
        out_shape=jax.ShapeDtypeStruct((NP, RESULTS, BH, BW), F32),
        in_specs=[hbm] * 8,
        out_specs=hbm,
        scratch_shapes=[
            vmem((1, NP), integers),
            vmem((1, NP), integers),
            each_stage((NP, 4, CHUNK, BW), F32),
            each_stage((NP, CHUNK, BW), integers),
            each_stage((NP, 5, CHUNK, BW), F32),
            each_stage((NP, CHUNK, BW), F32),
            each_stage((NP, CHUNK, BW), F32),
            each_stage((NP, CHUNK, BW), integers),
            vmem((NC, NP, NF, CHUNK, BW), F32),
            each_stage((NP, NF, CHUNK, BW), F32),
            each_stage((NP, NF, CHUNK, BW), F32),
            ids, ids, ids, ids,
            vmem((8, BW), integers),
            vmem((4, 8, BW), integers),
            pltpu.SMEM((8, BW), integers),
            pltpu.SMEM((4, 8, BW), integers),
            vmem((NS, 2, 2, 8, BW), F32),
            vmem((NS, 2, 2, 8, BW), F32),
            vmem((NC, NP, RESULTS, CHUNK, BW), F32),
            [vmem((NP, ROWS, BW), F32) for _ in TILE_FIELDS],
            [vmem((2, ROWS, BW), F32) for _ in TILE_FIELDS],
            dma((NC, 6)), dma((2,)), dma((NP,)), dma((NP,)), dma((2,)), dma((2,)), dma((5,)),
            dma((NC, NP)), dma((NC, NP)), dma((NC, NP)), dma((NC, NP)),
            dma((NS, 2)), dma((NS, 2)), dma((NC, NP)), dma((NC, NP)), dma((NC,)),
        ],
        compiler_params=pltpu.CompilerParams(
            collective_id=0, has_side_effects=True, vmem_limit_bytes=48 << 20
        ),
        cost_estimate=pl.CostEstimate(flops=100_000_000, bytes_accessed=6 << 20, transcendentals=0),
        name="ice_subcycles",
    )(*[
        pltpu.with_memory_space_constraint(array, pltpu.HBM)
        for array in (
            ocean_map[None], ice_map[None], ocean_state, land_mask,
            ice_motion, ice_mass, ice_strength, ice_mask,
        )
    ])
    return pl.pallas_call(
        to_slots,
        out_shape=(
            jax.ShapeDtypeStruct((NP, 5, BH, BW), F32),
            jax.ShapeDtypeStruct((NP, 2, BH, BW), F32),
        ),
        in_specs=[smem, smem, held],
        out_specs=(hbm, hbm),
        scratch_shapes=[
            dma((2, NP)),
        ],
        compiler_params=pltpu.CompilerParams(vmem_limit_bytes=16 << 20),
        name="to_slots",
    )(ocean_map, ice_map, held_back)


def solution(mesh):
    blocks = P(("gx", "gy"), None, None, None)
    layer = P(("gx", "gy"), None, None)
    slots = P(("gx", "gy"))
    return jax.shard_map(
        shards, mesh=mesh,
        in_specs=(blocks, layer, slots, blocks, layer, layer, layer, slots),
        out_specs=(blocks, blocks), check_vma=False,
    )
```
